256 devices in a mesh: lat: 8 (over x, y_lo), lon: 32 (over y_hi, z, core).
Axes of the slice: x: 4, y: 4 (y_hi: 2, y_lo: 2; y = y_hi * 2 + y_lo), z: 8, core: 2. Of those that a mesh axis runs over, the one named last changes fastest.
Arguments:
- fields: float32 [32, 1024, 1024], P('lat', 'lon'), as said below
- row_points: int32 [32], replicated, may hold values from 32 to 1024, as said below
- band_mask: int32 [8, 4], replicated, may hold values 0 or 1
- norm_gain: float32 [1024], replicated, may hold values from 0.1 to 1.9
- w_query: bfloat16 [1024, 1024], replicated, as said below
- w_key: bfloat16 [1024, 1024], replicated
- w_value: bfloat16 [1024, 1024], replicated, may hold values from -0.1875 to 0.1875
- w_out: bfloat16 [1024, 1024], replicated, may hold values from -0.1875 to 0.1875
Outputs:
- block_out: float32 [32, 1024, 1024], P('lat', 'lon')
The draws below stay inside these ranges and needn't reach their ends.
Inputs may be any that keep to these rules, and one draw needn't show every extreme that they name: fields: entries of order one to ten in magnitude, within -24 and 24. `row_points`: row r holds between half of its bound and its bound, where the bound is max(32, 1024 * (r + 1) // 32), and never fewer than 32; the last row holds 1024. `w_query`: entries of order 3 * 1024 ** -0.5.
All inputs are finite; a program needn't handle non-finite values.
Results may differ from the reference program's by a relative error of at most 0.0052.
Values may be sent and summed in bfloat16 or wider, within the bound.
No kernel may reach another device: no remote copies, remote signals or barrier semaphores. Data moves between devices by JAX's collectives and lax.ppermute only.
A program may use at most 128 MiB of HBM per device.

```python
import math
import jax
import jax.numpy as jnp
from jax import lax

D = 1024
HEADS = 16
HEAD_DIM = 64
AXIAL_HEADS = 8
REACH = 2
ROWS_DEV = 4
PTS_DEV = 32
ROWS = 32
SLOTS = 1024
N_LAT = 8
N_LON = 32


def draw_row_points(key, part):
    row_ids = jnp.arange(ROWS, dtype=jnp.int32)
    upper_bound = jnp.maximum(SLOTS * (row_ids + 1) // ROWS, N_LON)
    lowest = jnp.maximum(upper_bound // 2, N_LON)
    counts = jax.random.randint(key, (ROWS,), lowest, upper_bound + 1)
    return jnp.where(row_ids == ROWS - 1, SLOTS, counts).astype(jnp.int32)


def query_key_pair(key):
    base_query = jax.random.normal(jax.random.fold_in(key, 101), (D, D), jnp.float32)
    base_key = jax.random.normal(jax.random.fold_in(key, 202), (D, D), jnp.float32)
    query_part = jnp.clip(base_query, -6.0, 6.0) * (3.0 / math.sqrt(D))
    free_key = jnp.clip(base_key, -6.0, 6.0) / math.sqrt(D)
    key_part = free_key
    return (query_part, key_part)


def draw_w_query(key, part):
    return query_key_pair(key)[0].astype(jnp.bfloat16)


def draw_w_key(key, part):
    return query_key_pair(key)[1].astype(jnp.bfloat16)


def draw_fields(key, part):
    base = jax.random.normal(jax.random.fold_in(key, 11), (ROWS, SLOTS, D), jnp.float32)
    return jnp.clip(base, -6.0, 6.0)


def touch_ends(values, key, smallest, high):
    extent = values.shape
    spot = [jax.random.randint(jax.random.fold_in(key, axis), (), 0, extent[axis]) for axis in range(len(extent))]
    values = values.at[tuple(spot)].set(smallest)
    longest = extent.index(max(extent))
    spot[longest] = (spot[longest] + 1) % extent[longest]
    return values.at[tuple(spot)].set(high)


def normal_values(stream_key, shape, width, bound, kind=jnp.bfloat16):
    drawn = width * jax.random.normal(stream_key, shape, jnp.float32)
    return jnp.clip(drawn, min=-bound, max=bound).astype(kind)


def setup_inputs(seed: int = 0) -> dict:
    streams_of = jax.random.split(jax.random.key(seed), 9)
    fields = draw_fields(jax.random.fold_in(streams_of[8], 71), 0)
    row_points = draw_row_points(jax.random.fold_in(streams_of[8], 71), 0)
    band_mask = touch_ends((jax.random.randint(streams_of[2], (N_LAT, 2 * REACH), 0, 4) < 3).astype(jnp.int32), jax.random.fold_in(streams_of[2], 1), 0, 1)
    norm_gain = jnp.clip(1.0 + 0.18 * jax.random.normal(streams_of[3], (D,), jnp.float32), 0.1, 1.9)
    w_query = draw_w_query(jax.random.fold_in(streams_of[8], 71), 0)
    w_key = draw_w_key(jax.random.fold_in(streams_of[8], 71), 0)
    w_value = normal_values(streams_of[6], (D, D), D ** -0.5, 0.1875)
    w_out = normal_values(streams_of[7], (D, D), D ** -0.5, 0.1875)
    return dict(fields=fields, row_points=row_points, band_mask=band_mask, norm_gain=norm_gain, w_query=w_query, w_key=w_key, w_value=w_value, w_out=w_out)


EPS = 1e-05

def live_slots(row_points):
    slot_ids = jnp.arange(SLOTS, dtype=jnp.int32)
    owner_ids = slot_ids // PTS_DEV
    within = slot_ids % PTS_DEV
    live_counts = row_points[:, None] // N_LON + (owner_ids[None, :] < row_points[:, None] % N_LON).astype(jnp.int32)
    return within[None, :] < live_counts

def softmax_mix(scores, key_live, values):
    scores = jnp.where(key_live, scores, -jnp.inf)
    row_peak = lax.optimization_barrier(jnp.max(scores, axis=-1, keepdims=True))
    weights = jnp.exp(scores - row_peak)
    weight_sum = lax.optimization_barrier(jnp.sum(weights, axis=-1))
    rounded = lax.optimization_barrier(weights.astype(jnp.bfloat16))
    mixed_heads = jnp.einsum('hqk,khd->qhd', rounded.astype(jnp.float32), values.astype(jnp.float32))
    return mixed_heads / jnp.transpose(weight_sum)[:, :, None]

def reference(fields, row_points, band_mask, norm_gain, w_query, w_key, w_value, w_out):
    score_scale = HEAD_DIM ** (-0.5)
    band_heads = HEADS - AXIAL_HEADS
    row_mean = lax.optimization_barrier(jnp.mean(fields, axis=-1, keepdims=True))
    centred = fields - row_mean
    row_var = lax.optimization_barrier(jnp.mean(centred * centred, axis=-1, keepdims=True))
    normed = (centred * lax.rsqrt(row_var + EPS) * norm_gain).astype(jnp.bfloat16).reshape(ROWS * SLOTS, D)
    queries = jnp.dot(normed, w_query, preferred_element_type=jnp.float32).astype(jnp.bfloat16).reshape(ROWS, SLOTS, HEADS, HEAD_DIM)
    key_heads = jnp.dot(normed, w_key, preferred_element_type=jnp.float32).astype(jnp.bfloat16).reshape(ROWS, SLOTS, HEADS, HEAD_DIM)
    value_heads = jnp.dot(normed, w_value, preferred_element_type=jnp.float32).astype(jnp.bfloat16).reshape(ROWS, SLOTS, HEADS, HEAD_DIM)
    live = live_slots(row_points)

    def axial_row(inputs):
        row_query, row_key, row_value, row_live = inputs
        scores = jnp.einsum('qhd,khd->hqk', row_query.astype(jnp.float32), row_key.astype(jnp.float32)) * score_scale
        return softmax_mix(scores, row_live[None, None, :], row_value)
    axial_out = lax.map(axial_row, (queries[:, :, :AXIAL_HEADS], key_heads[:, :, :AXIAL_HEADS], value_heads[:, :, :AXIAL_HEADS], live))
    pad_rows = REACH * ROWS_DEV
    band_query = queries[:, :, AXIAL_HEADS:]
    key_pad = jnp.pad(key_heads[:, :, AXIAL_HEADS:], ((pad_rows, pad_rows), (0, 0), (0, 0), (0, 0)))
    value_pad = jnp.pad(value_heads[:, :, AXIAL_HEADS:], ((pad_rows, pad_rows), (0, 0), (0, 0), (0, 0)))
    live_pad = jnp.pad(live, ((pad_rows, pad_rows), (0, 0)))
    window = jnp.arange(2 * REACH + 1, dtype=jnp.int32) - REACH
    lat_ids = jnp.arange(N_LAT, dtype=jnp.int32)
    column = jnp.clip(jnp.where(window < 0, window + REACH, window + REACH - 1), 0, 2 * REACH - 1).astype(jnp.int32)
    source = lat_ids[:, None] + window[None, :]
    inside = (source >= 0) & (source < N_LAT)
    picked = jnp.take_along_axis(band_mask, jnp.broadcast_to(column[None, :], (N_LAT, 2 * REACH + 1)), axis=1)
    allowed = (window[None, :] == 0) | inside & (picked == 1)
    window_rows = (2 * REACH + 1) * ROWS_DEV
    zero_index = jnp.zeros((), jnp.int32)

    def band_tile(tile_index):
        tile_index = tile_index.astype(jnp.int32)
        lat_band = (tile_index // N_LON).astype(jnp.int32)
        lon_tile = (tile_index % N_LON).astype(jnp.int32)
        first_row = (lat_band * ROWS_DEV).astype(jnp.int32)
        first_slot = (lon_tile * PTS_DEV).astype(jnp.int32)
        tile_query = lax.dynamic_slice(band_query, (first_row, first_slot, zero_index, zero_index), (ROWS_DEV, PTS_DEV, band_heads, HEAD_DIM)).reshape(ROWS_DEV * PTS_DEV, band_heads, HEAD_DIM)
        tile_key = lax.dynamic_slice(key_pad, (first_row, first_slot, zero_index, zero_index), (window_rows, PTS_DEV, band_heads, HEAD_DIM)).reshape(window_rows * PTS_DEV, band_heads, HEAD_DIM)
        tile_value = lax.dynamic_slice(value_pad, (first_row, first_slot, zero_index, zero_index), (window_rows, PTS_DEV, band_heads, HEAD_DIM)).reshape(window_rows * PTS_DEV, band_heads, HEAD_DIM)
        tile_live = lax.dynamic_slice(live_pad, (first_row, first_slot), (window_rows, PTS_DEV))
        tile_allow = jnp.repeat(allowed[lat_band], ROWS_DEV)
        key_live = (tile_live & tile_allow[:, None]).reshape(window_rows * PTS_DEV)
        scores = jnp.einsum('qhd,khd->hqk', tile_query.astype(jnp.float32), tile_key.astype(jnp.float32)) * score_scale
        return softmax_mix(scores, key_live[None, None, :], tile_value)
    band_tiles = lax.map(band_tile, jnp.arange(N_LAT * N_LON, dtype=jnp.int32))
    band_out = band_tiles.reshape(N_LAT, N_LON, ROWS_DEV, PTS_DEV, band_heads, HEAD_DIM).transpose(0, 2, 1, 3, 4, 5).reshape(ROWS, SLOTS, band_heads, HEAD_DIM)
    mixed_heads = jnp.concatenate([axial_out, band_out], axis=2).reshape(ROWS * SLOTS, D).astype(jnp.bfloat16)
    projected = jnp.dot(mixed_heads, w_out, preferred_element_type=jnp.float32).reshape(ROWS, SLOTS, D)
    return jnp.where(live[:, :, None], fields + projected, 0.0)
```

```python
import functools

import jax
import jax.numpy as jnp
from jax import lax
from jax.experimental import pallas as pl
from jax.experimental.pallas import tpu as pltpu
from jax.sharding import PartitionSpec as P

HEADS = 16
HEAD_DIM = 64
AXIAL_HEADS = 8
REACH = 2
EPS = 1e-05
DEAD = -1e30
PAIR = 2 * HEAD_DIM
SCALE = HEAD_DIM**-0.5
OFFSETS = (-2, -1, 1, 2)

VMEM = pl.BlockSpec(memory_space=pltpu.VMEM)
SMEM = pl.BlockSpec(memory_space=pltpu.SMEM)
PARAMS = pltpu.CompilerParams(vmem_limit_bytes=48 * 1024 * 1024)


def dot(a, b):
    return jnp.dot(a, b, preferred_element_type=jnp.float32)


def dot_t(a, b):
    return lax.dot_general(a, b, (((1,), (1,)), ((), ())), preferred_element_type=jnp.float32)


def half_roll(value):
    return pltpu.roll(value, HEAD_DIM, 1)


def low_half(shape):
    return lax.broadcasted_iota(jnp.int32, shape, 1) < HEAD_DIM


def live_count(points, tile, tiles):
    return points // tiles + (tile < points % tiles).astype(jnp.int32)


def norm_kernel(fields_ref, gain_ref, out_ref):
    rows, slots, width = fields_ref.shape
    values = fields_ref[...].reshape(rows * slots, width)
    mean = jnp.mean(values, axis=-1, keepdims=True)
    centred = values - mean
    var = jnp.mean(centred * centred, axis=-1, keepdims=True)
    out_ref[...] = (centred * lax.rsqrt(var + EPS) * gain_ref[...]).astype(jnp.bfloat16)


def axial_project_kernel(lon_count, own_ref, peer_ref, wq_ref, wk_ref, wv_ref, out_ref):
    core = lax.rem(lax.axis_index("lon"), 2)
    tokens = own_ref.shape[0]
    slots = out_ref.shape[1] // 3
    rows = tokens // slots
    heads = AXIAL_HEADS // 2
    width = heads * HEAD_DIM
    columns = pl.ds(pl.multiple_of(core * width, width), width)
    both = jnp.concatenate([own_ref[...], peer_ref[...]], axis=0)
    query = dot(both, wq_ref[:, columns])
    key = dot(both, wk_ref[:, columns])
    value = dot(both, wv_ref[:, columns])
    low = low_half((2 * tokens, PAIR))
    low_v = low_half((tokens, PAIR))
    for pair in range(heads // 2):
        span = slice(pair * PAIR, (pair + 1) * PAIR)
        q, k = query[:, span], key[:, span]
        v_own, v_peer = value[:tokens, span], value[tokens:, span]
        qk = (jnp.where(low, q, half_roll(k)), jnp.where(low, half_roll(q), k))
        v = (jnp.where(low_v, v_own, half_roll(v_peer)), jnp.where(low_v, half_roll(v_own), v_peer))
        for side in range(2):
            qk_side = qk[side].astype(jnp.bfloat16)
            v_side = v[side].astype(jnp.bfloat16)
            for row in range(rows):
                item = row * heads + pair * 2 + side
                part = slice(row * slots, (row + 1) * slots)
                part_peer = slice(tokens + row * slots, tokens + (row + 1) * slots)
                out_ref[item, 0:slots, :] = qk_side[part]
                out_ref[item, slots : 2 * slots, :] = qk_side[part_peer]
                out_ref[item, 2 * slots : 3 * slots, :] = v_side[part]


def axial_kernel(lon_count, points_ref, in_ref, out_ref):
    lon = lax.axis_index("lon")
    core = lax.rem(lon, 2)
    chip = lon // 2
    chips, third, _ = in_ref.shape
    slots = third // 3
    rows = chips // (AXIAL_HEADS // 2)
    points = points_ref[lax.axis_index("lat") * rows + chip // (AXIAL_HEADS // 2)]
    keys = chips * 2 * slots
    query_key = in_ref[:, : 2 * slots, :].astype(jnp.float32).reshape(keys, PAIR)
    lane = lax.broadcasted_iota(jnp.int32, (keys, PAIR), 1)
    index = lax.broadcasted_iota(jnp.int32, (keys, PAIR), 0)
    half = lax.rem(index // slots, 2)
    tile = 2 * (index // (2 * slots)) + jnp.where(half == 0, core, 1 - core)
    live = lax.rem(index, slots) < points // lon_count + (tile < points % lon_count).astype(jnp.int32)
    bias = jnp.where(live, 0.0, DEAD)
    one_hot = (lane == HEAD_DIM).astype(jnp.float32)
    low = lane < HEAD_DIM
    query = jnp.where(low, query_key * SCALE, one_hot).astype(jnp.bfloat16)
    key = jnp.where(low, half_roll(query_key), one_hot * bias).astype(jnp.bfloat16)
    key = key.reshape(chips, 2, slots, PAIR)
    key_own = key[:, 0].reshape(chips * slots, PAIR)
    key_peer = key[:, 1].reshape(chips * slots, PAIR)
    value = in_ref[:, 2 * slots :, :].reshape(chips * slots, PAIR)
    block = 4 * 2 * slots
    low_block = low_half((block, PAIR))
    low_out = low_half((slots, PAIR))
    for step in range(keys // block):
        q = query[step * block : (step + 1) * block]
        s_own = dot_t(q, key_own)
        s_peer = dot_t(q, key_peer)
        peak = jnp.maximum(
            jnp.max(s_own, axis=-1, keepdims=True), jnp.max(s_peer, axis=-1, keepdims=True)
        )
        e_own = jnp.exp(s_own - peak)
        e_peer = jnp.exp(s_peer - peak)
        total = jnp.sum(e_own, axis=-1, keepdims=True) + jnp.sum(e_peer, axis=-1, keepdims=True)
        mixed = dot(e_own.astype(jnp.bfloat16), value)
        mixed_peer = half_roll(dot(e_peer.astype(jnp.bfloat16), value))
        mixed = jnp.where(low_block, mixed + mixed_peer, 0.0) / total
        for chip_of in range(4):
            first = mixed[chip_of * 2 * slots : chip_of * 2 * slots + slots]
            second = mixed[chip_of * 2 * slots + slots : (chip_of + 1) * 2 * slots]
            out_ref[step * 4 + chip_of] = jnp.where(low_out, first, half_roll(second)).astype(
                jnp.bfloat16
            )


def band_kernel(
    lat_count, lon_count, points_ref, mask_ref, own_ref, m2_ref, m1_ref, p1_ref, p2_ref,
    wq_ref, wk_ref, wv_ref, out_ref,
):
    lat = lax.axis_index("lat")
    lon = lax.axis_index("lon")
    tokens = own_ref.shape[0]
    slots = 32
    rows = tokens // slots
    first = AXIAL_HEADS * HEAD_DIM
    bands = (0,) + OFFSETS
    everything = jnp.concatenate(
        [own_ref[...], m2_ref[...], m1_ref[...], p1_ref[...], p2_ref[...]], axis=0
    )
    keys = everything.shape[0]
    key = dot(everything, wk_ref[:, first:]).astype(jnp.bfloat16)
    value = dot(everything, wv_ref[:, first:]).astype(jnp.bfloat16)
    query = dot(own_ref[...], wq_ref[:, first:]).astype(jnp.bfloat16)
    slot = lax.broadcasted_iota(jnp.int32, (slots, PAIR), 0)
    blocks = []
    for offset in bands:
        source = lat + offset
        held = jnp.clip(source, 0, lat_count - 1)
        if offset == 0:
            allowed = jnp.int32(1)
        else:
            column = offset + REACH if offset < 0 else offset + REACH - 1
            inside = (source >= 0) & (source < lat_count)
            allowed = jnp.where(inside & (mask_ref[lat, column] == 1), 1, 0)
        for row in range(rows):
            count = live_count(points_ref[held * rows + row], lon, lon_count) * allowed
            blocks.append(jnp.where(slot < count, 0.0, DEAD))
    bias = jnp.concatenate(blocks, axis=0).astype(jnp.bfloat16)
    lane_k = lax.broadcasted_iota(jnp.int32, (keys, PAIR), 1)
    lane_q = lax.broadcasted_iota(jnp.int32, (tokens, PAIR), 1)
    zero_k = jnp.zeros((keys, PAIR), jnp.bfloat16)
    low_o = lane_q < HEAD_DIM
    for pair in range((HEADS - AXIAL_HEADS) // 2):
        span = slice(pair * PAIR, (pair + 1) * PAIR)
        q, k, v = query[:, span] * jnp.bfloat16(SCALE), key[:, span], value[:, span]
        outs = []
        for side in range(2):
            spare = HEAD_DIM if side == 0 else 0
            mine_q = (lane_q < HEAD_DIM) if side == 0 else (lane_q >= HEAD_DIM)
            mine_k = (lane_k < HEAD_DIM) if side == 0 else (lane_k >= HEAD_DIM)
            q_side = jnp.where(mine_q, q, (lane_q == spare).astype(jnp.bfloat16))
            k_side = jnp.where(mine_k, k, jnp.where(lane_k == spare, bias, zero_k))
            scores = dot_t(q_side, k_side)
            peak = jnp.max(scores, axis=-1, keepdims=True)
            weights = jnp.exp(scores - peak)
            total = jnp.sum(weights, axis=-1, keepdims=True)
            outs.append(dot(weights.astype(jnp.bfloat16), v) / total)
        out_ref[:, span] = jnp.where(low_o, outs[0], outs[1]).astype(jnp.bfloat16)


def band_out_kernel(fields_ref, band_ref, w_ref, out_ref):
    rows, slots, width = fields_ref.shape
    first = AXIAL_HEADS * HEAD_DIM
    out_ref[...] = fields_ref[...].reshape(rows * slots, width) + dot(band_ref[...], w_ref[first:, :])


def finish_kernel(lon_count, points_ref, sum_ref, mine_ref, other_ref, w_ref, out_ref):
    lon = lax.axis_index("lon")
    core = lax.rem(lon, 2)
    rows, slots, width = out_ref.shape
    heads = AXIAL_HEADS // 2
    low = low_half((slots, PAIR))
    mine_rows, other_rows = [], []
    for row in range(rows):
        mine, other = [], []
        for pair in range(heads // 2):
            item = row * heads + pair * 2
            a = mine_ref[item].astype(jnp.float32)
            b = mine_ref[item + 1].astype(jnp.float32)
            mine.append(jnp.where(low, a, half_roll(b)))
            a = other_ref[item].astype(jnp.float32)
            b = other_ref[item + 1].astype(jnp.float32)
            other.append(jnp.where(low, half_roll(a), b))
        mine_rows.append(jnp.concatenate(mine, axis=1))
        other_rows.append(jnp.concatenate(other, axis=1))
    mine = jnp.concatenate(mine_rows, axis=0).astype(jnp.bfloat16)
    other = jnp.concatenate(other_rows, axis=0).astype(jnp.bfloat16)
    depth = heads * HEAD_DIM
    mine_w = w_ref[pl.ds(pl.multiple_of(core * depth, depth), depth), :]
    other_w = w_ref[pl.ds(pl.multiple_of((1 - core) * depth, depth), depth), :]
    result = sum_ref[...] + dot(mine, mine_w) + dot(other, other_w)
    slot = lax.broadcasted_iota(jnp.int32, (slots, width), 0)
    for row in range(rows):
        count = live_count(points_ref[lax.axis_index("lat") * rows + row], lon, lon_count)
        part = result[row * slots : (row + 1) * slots]
        out_ref[row] = jnp.where(slot < count, part, 0.0)


def call(kernel, shape, dtype, specs):
    return pl.pallas_call(
        kernel,
        out_shape=jax.ShapeDtypeStruct(shape, dtype),
        in_specs=specs,
        out_specs=VMEM,
        compiler_params=PARAMS,
    )


def on_device(fields, row_points, band_mask, norm_gain, w_query, w_key, w_value, w_out):
    rows, slots, width = fields.shape
    lat_count = lax.axis_size("lat")
    lon_count = lax.axis_size("lon")
    tokens = rows * slots
    chips = lon_count // 2
    bf16 = jnp.bfloat16
    groups = [[2 * chip + core for chip in range(chips)] for core in range(2)]
    swap = [(place, place + 1 - 2 * (place % 2)) for place in range(lon_count)]

    normed = call(norm_kernel, (tokens, width), bf16, [VMEM, VMEM])(
        fields, norm_gain.reshape(1, width)
    )
    peer = lax.ppermute(normed, "lon", swap)
    near = [
        lax.ppermute(
            normed, "lat", [(place, (place - offset) % lat_count) for place in range(lat_count)]
        )
        for offset in OFFSETS
    ]
    packed = call(
        functools.partial(axial_project_kernel, lon_count), (chips, 3 * slots, PAIR), bf16, [VMEM] * 5
    )(normed, peer, w_query, w_key, w_value)
    row_head = lax.all_to_all(packed, "lon", 0, 0, axis_index_groups=groups, tiled=True)
    axial = call(
        functools.partial(axial_kernel, lon_count), (chips, slots, PAIR), bf16, [SMEM, VMEM]
    )(row_points, row_head)
    mine = lax.all_to_all(axial, "lon", 0, 0, axis_index_groups=groups, tiled=True)
    other = lax.ppermute(mine, "lon", swap)
    band = call(
        functools.partial(band_kernel, lat_count, lon_count),
        (tokens, (HEADS - AXIAL_HEADS) * HEAD_DIM),
        bf16,
        [SMEM, SMEM] + [VMEM] * 8,
    )(row_points, band_mask, normed, *near, w_query, w_key, w_value)
    summed = call(band_out_kernel, (tokens, width), jnp.float32, [VMEM] * 3)(fields, band, w_out)
    return call(
        functools.partial(finish_kernel, lon_count), (rows, slots, width), jnp.float32, [SMEM] + [VMEM] * 4
    )(row_points, summed, mine, other, w_out)


def solution(mesh):
    in_specs = (P("lat", "lon", None), P(), P(), P(), P(), P(), P(), P())
    out_specs = P("lat", "lon", None)
    return jax.shard_map(
        on_device, mesh=mesh, in_specs=in_specs, out_specs=out_specs, check_vma=False
    )
```

```python
import functools

import jax
import jax.numpy as jnp
from jax import lax
from jax.experimental import pallas as pl
from jax.experimental.pallas import tpu as pltpu
from jax.sharding import PartitionSpec as P

HEADS = 16
HEAD_DIM = 64
AXIAL_HEADS = 8
REACH = 2
EPS = 1e-05
DEAD = -1e30
PAIR = 2 * HEAD_DIM
SCALE = HEAD_DIM**-0.5
OFFSETS = (-2, -1, 1, 2)
BAND_FLOPS = 20_000_000_000
BAND_OUT_FLOPS = 20_000_000_000

VMEM = pl.BlockSpec(memory_space=pltpu.VMEM)
SMEM = pl.BlockSpec(memory_space=pltpu.SMEM)
HBM = pl.BlockSpec(memory_space=pltpu.HBM)
ANY = pl.BlockSpec(memory_space=pl.ANY)


def dot(a, b):
    return jnp.dot(a, b, preferred_element_type=jnp.float32)


def dot_t(a, b):
    return lax.dot_general(a, b, (((1,), (1,)), ((), ())), preferred_element_type=jnp.float32)


def half_roll(value):
    return pltpu.roll(value, HEAD_DIM, 1)


def low_half(shape):
    return lax.broadcasted_iota(jnp.int32, shape, 1) < HEAD_DIM


def live_count(points, tile, tiles):
    return points // tiles + (tile < points % tiles).astype(jnp.int32)


def norm_kernel(
    fields_hbm, gain_hbm, wq_hbm, wk_hbm, wv_hbm, out_ref, weights_ref, fields_ref, gain_ref, sems
):
    core = lax.rem(lax.axis_index("lon"), 2)
    width = weights_ref.shape[2]
    columns = pl.ds(pl.multiple_of(core * width, width), width)
    first = [
        pltpu.make_async_copy(fields_hbm, fields_ref, sems.at[0]),
        pltpu.make_async_copy(gain_hbm, gain_ref, sems.at[1]),
    ]
    rest = [
        pltpu.make_async_copy(hbm.at[:, columns], weights_ref.at[place], sems.at[2 + place])
        for place, hbm in enumerate((wq_hbm, wk_hbm, wv_hbm))
    ]
    for copy in first + rest:
        copy.start()
    for copy in first:
        copy.wait()
    rows, slots, width = fields_ref.shape
    values = fields_ref[...].reshape(rows * slots, width)
    mean = jnp.mean(values, axis=-1, keepdims=True)
    centred = values - mean
    var = jnp.mean(centred * centred, axis=-1, keepdims=True)
    out_ref[...] = (centred * lax.rsqrt(var + EPS) * gain_ref[...]).astype(jnp.bfloat16)
    for copy in rest:
        copy.wait()


def axial_project_kernel(own_ref, peer_ref, weights_ref, out_ref):
    tokens = own_ref.shape[0]
    slots = out_ref.shape[1] // 3
    rows = tokens // slots
    heads = AXIAL_HEADS // 2
    both = jnp.concatenate([own_ref[...], peer_ref[...]], axis=0)
    query = dot(both, weights_ref[0])
    key = dot(both, weights_ref[1])
    value = dot(both, weights_ref[2])
    low = low_half((2 * tokens, PAIR))
    low_v = low_half((tokens, PAIR))
    for pair in range(heads // 2):
        span = slice(pair * PAIR, (pair + 1) * PAIR)
        q, k = query[:, span], key[:, span]
        v_own, v_peer = value[:tokens, span], value[tokens:, span]
        qk = (jnp.where(low, q, half_roll(k)), jnp.where(low, half_roll(q), k))
        v = (jnp.where(low_v, v_own, half_roll(v_peer)), jnp.where(low_v, half_roll(v_own), v_peer))
        for side in range(2):
            qk_side = qk[side].astype(jnp.bfloat16)
            v_side = v[side].astype(jnp.bfloat16)
            for row in range(rows):
                item = row * heads + pair * 2 + side
                part = slice(row * slots, (row + 1) * slots)
                part_peer = slice(tokens + row * slots, tokens + (row + 1) * slots)
                out_ref[item, 0:slots, :] = qk_side[part]
                out_ref[item, slots : 2 * slots, :] = qk_side[part_peer]
                out_ref[item, 2 * slots : 3 * slots, :] = v_side[part]


def axial_kernel(lon_count, points_ref, in_ref, band_ref, out_ref):
    lon = lax.axis_index("lon")
    core = lax.rem(lon, 2)
    chip = lon // 2
    chips, third, _ = in_ref.shape
    slots = third // 3
    rows = chips // (AXIAL_HEADS // 2)
    points = points_ref[lax.axis_index("lat") * rows + chip // (AXIAL_HEADS // 2)]
    keys = chips * 2 * slots
    query_key = in_ref[:, : 2 * slots, :].astype(jnp.float32).reshape(keys, PAIR)
    lane = lax.broadcasted_iota(jnp.int32, (keys, PAIR), 1)
    index = lax.broadcasted_iota(jnp.int32, (keys, PAIR), 0)
    half = lax.rem(index // slots, 2)
    tile = 2 * (index // (2 * slots)) + jnp.where(half == 0, core, 1 - core)
    live = lax.rem(index, slots) < points // lon_count + (tile < points % lon_count).astype(jnp.int32)
    bias = jnp.where(live, 0.0, DEAD)
    one_hot = (lane == HEAD_DIM).astype(jnp.float32)
    low = lane < HEAD_DIM
    query = jnp.where(low, query_key * SCALE, one_hot).astype(jnp.bfloat16)
    key = jnp.where(low, half_roll(query_key), one_hot * bias).astype(jnp.bfloat16)
    key = key.reshape(chips, 2, slots, PAIR)
    key_own = key[:, 0].reshape(chips * slots, PAIR)
    key_peer = key[:, 1].reshape(chips * slots, PAIR)
    value = in_ref[:, 2 * slots :, :].reshape(chips * slots, PAIR)
    block = 4 * 2 * slots
    low_block = low_half((block, PAIR))
    low_out = low_half((slots, PAIR))
    for step in range(keys // block):
        q = query[step * block : (step + 1) * block]
        s_own = dot_t(q, key_own)
        s_peer = dot_t(q, key_peer)
        peak = jnp.maximum(
            jnp.max(s_own, axis=-1, keepdims=True), jnp.max(s_peer, axis=-1, keepdims=True)
        )
        e_own = jnp.exp(s_own - peak)
        e_peer = jnp.exp(s_peer - peak)
        total = jnp.sum(e_own, axis=-1, keepdims=True) + jnp.sum(e_peer, axis=-1, keepdims=True)
        mixed = dot(e_own.astype(jnp.bfloat16), value)
        mixed_peer = half_roll(dot(e_peer.astype(jnp.bfloat16), value))
        mixed = jnp.where(low_block, mixed + mixed_peer, 0.0) / total
        for chip_of in range(4):
            first = mixed[chip_of * 2 * slots : chip_of * 2 * slots + slots]
            second = mixed[chip_of * 2 * slots + slots : (chip_of + 1) * 2 * slots]
            out_ref[step * 4 + chip_of] = jnp.where(low_out, first, half_roll(second)).astype(
                jnp.bfloat16
            )


def band_kernel(
    lat_count, lon_count, points_ref, mask_ref, own_ref, m2_ref, m1_ref, p1_ref, p2_ref,
    wq_hbm, wk_hbm, wv_hbm, out_ref, wq_ref, wkv_ref, sems,
):
    pairs = (HEADS - AXIAL_HEADS) // 2
    first = AXIAL_HEADS * HEAD_DIM
    copies = []
    for pair in range(pairs):
        columns = pl.ds(first + pair * PAIR, PAIR)
        copies.append(
            [
                pltpu.make_async_copy(wk_hbm.at[:, columns], wkv_ref.at[pair, :, pl.ds(0, PAIR)], sems.at[pair, 0]),
                pltpu.make_async_copy(wv_hbm.at[:, columns], wkv_ref.at[pair, :, pl.ds(PAIR, PAIR)], sems.at[pair, 1]),
                pltpu.make_async_copy(wq_hbm.at[:, columns], wq_ref.at[pair], sems.at[pair, 2]),
            ]
        )
    for group in copies:
        for copy in group:
            copy.start()
    lat = lax.axis_index("lat")
    lon = lax.axis_index("lon")
    tokens = own_ref.shape[0]
    slots = 32
    rows = tokens // slots
    bands = (0,) + OFFSETS
    own = own_ref[...]
    everything = jnp.concatenate([own, m2_ref[...], m1_ref[...], p1_ref[...], p2_ref[...]], axis=0)
    keys = everything.shape[0]
    slot = lax.broadcasted_iota(jnp.int32, (slots, PAIR), 0)
    blocks = []
    for offset in bands:
        source = lat + offset
        held = jnp.clip(source, 0, lat_count - 1)
        if offset == 0:
            allowed = jnp.int32(1)
        else:
            column = offset + REACH if offset < 0 else offset + REACH - 1
            inside = (source >= 0) & (source < lat_count)
            allowed = jnp.where(inside & (mask_ref[column, lat] == 1), 1, 0)
        for row in range(rows):
            count = live_count(points_ref[held * rows + row], lon, lon_count) * allowed
            blocks.append(jnp.where(slot < count, 0.0, DEAD))
    bias = jnp.concatenate(blocks, axis=0).astype(jnp.bfloat16)
    lane_k = lax.broadcasted_iota(jnp.int32, (keys, PAIR), 1)
    lane_q = lax.broadcasted_iota(jnp.int32, (tokens, PAIR), 1)
    zero_k = jnp.zeros((keys, PAIR), jnp.bfloat16)
    low_o = lane_q < HEAD_DIM
    for pair in range(pairs):
        for copy in copies[pair]:
            copy.wait()
        kv = dot(everything, wkv_ref[pair]).astype(jnp.bfloat16)
        k, v = kv[:, :PAIR], kv[:, PAIR:]
        q = dot(own, wq_ref[pair]).astype(jnp.bfloat16) * jnp.bfloat16(SCALE)
        outs = []
        for side in range(2):
            spare = HEAD_DIM if side == 0 else 0
            mine_q = (lane_q < HEAD_DIM) if side == 0 else (lane_q >= HEAD_DIM)
            mine_k = (lane_k < HEAD_DIM) if side == 0 else (lane_k >= HEAD_DIM)
            q_side = jnp.where(mine_q, q, (lane_q == spare).astype(jnp.bfloat16))
            k_side = jnp.where(mine_k, k, jnp.where(lane_k == spare, bias, zero_k))
            scores = dot_t(q_side, k_side)
            peak = jnp.max(scores, axis=-1, keepdims=True)
            weights = jnp.exp(scores - peak)
            total = jnp.sum(weights, axis=-1, keepdims=True)
            outs.append(dot(weights.astype(jnp.bfloat16), v) / total)
        out_ref[:, pair * PAIR : (pair + 1) * PAIR] = jnp.where(low_o, outs[0], outs[1]).astype(
            jnp.bfloat16
        )


def band_out_kernel(fields_hbm, band_ref, w_hbm, out_ref, axial_w_ref, fields_ref, w_ref, sems):
    rows, slots, width = fields_ref.shape
    depth = w_ref.shape[0]
    copies = [
        pltpu.make_async_copy(w_hbm.at[pl.ds(depth, depth)], w_ref, sems.at[0]),
        pltpu.make_async_copy(fields_hbm, fields_ref, sems.at[1]),
        pltpu.make_async_copy(w_hbm.at[pl.ds(0, depth)], axial_w_ref, sems.at[2]),
    ]
    for copy in copies:
        copy.start()
    for copy in copies[:2]:
        copy.wait()
    out_ref[...] = fields_ref[...].reshape(rows * slots, width) + dot(band_ref[...], w_ref[...])
    copies[2].wait()


def finish_kernel(lon_count, points_ref, sum_ref, mine_ref, other_ref, w_ref, out_ref):
    lon = lax.axis_index("lon")
    core = lax.rem(lon, 2)
    rows, slots, width = out_ref.shape
    heads = AXIAL_HEADS // 2
    low = low_half((slots, PAIR))
    mine_rows, other_rows = [], []
    for row in range(rows):
        mine, other = [], []
        for pair in range(heads // 2):
            item = row * heads + pair * 2
            a = mine_ref[item].astype(jnp.float32)
            b = mine_ref[item + 1].astype(jnp.float32)
            mine.append(jnp.where(low, a, half_roll(b)))
            a = other_ref[item].astype(jnp.float32)
            b = other_ref[item + 1].astype(jnp.float32)
            other.append(jnp.where(low, half_roll(a), b))
        mine_rows.append(jnp.concatenate(mine, axis=1))
        other_rows.append(jnp.concatenate(other, axis=1))
    mine = jnp.concatenate(mine_rows, axis=0).astype(jnp.bfloat16)
    other = jnp.concatenate(other_rows, axis=0).astype(jnp.bfloat16)
    depth = heads * HEAD_DIM
    mine_w = w_ref[pl.ds(pl.multiple_of(core * depth, depth), depth), :]
    other_w = w_ref[pl.ds(pl.multiple_of((1 - core) * depth, depth), depth), :]
    result = sum_ref[...] + dot(mine, mine_w) + dot(other, other_w)
    slot = lax.broadcasted_iota(jnp.int32, (slots, width), 0)
    for row in range(rows):
        count = live_count(points_ref[lax.axis_index("lat") * rows + row], lon, lon_count)
        part = result[row * slots : (row + 1) * slots]
        out_ref[row] = jnp.where(slot < count, part, 0.0)


def call(kernel, shapes, specs, scratch=(), flops=0):
    return pl.pallas_call(
        kernel,
        out_shape=[jax.ShapeDtypeStruct(shape, dtype) for shape, dtype in shapes],
        in_specs=specs,
        out_specs=[VMEM] * len(shapes),
        scratch_shapes=scratch,
        compiler_params=pltpu.CompilerParams(vmem_limit_bytes=24 * 1024 * 1024),
        cost_estimate=pl.CostEstimate(flops=flops, transcendentals=0, bytes_accessed=0) if flops else None,
    )


def on_device(fields, row_points, band_mask, norm_gain, w_query, w_key, w_value, w_out):
    rows, slots, width = fields.shape
    lat_count = lax.axis_size("lat")
    lon_count = lax.axis_size("lon")
    tokens = rows * slots
    chips = lon_count // 2
    axial_width = AXIAL_HEADS * HEAD_DIM
    band_width = (HEADS - AXIAL_HEADS) * HEAD_DIM
    pairs = band_width // PAIR
    bf16, f32 = jnp.bfloat16, jnp.float32
    groups = [[2 * chip + core for chip in range(chips)] for core in range(2)]
    swap = [(place, place + 1 - 2 * (place % 2)) for place in range(lon_count)]

    def in_hbm(*arrays):
        return [pltpu.with_memory_space_constraint(array, pltpu.HBM) for array in arrays]

    normed, weights = call(
        norm_kernel,
        [((tokens, width), bf16), ((3, width, axial_width // 2), bf16)],
        [HBM] * 5,
        [
            pltpu.VMEM((rows, slots, width), f32),
            pltpu.VMEM((1, width), f32),
            pltpu.SemaphoreType.DMA((5,)),
        ],
    )(*in_hbm(fields, norm_gain.reshape(1, width), w_query, w_key, w_value))
    peer = lax.ppermute(normed, "lon", swap)
    near = [
        lax.ppermute(
            normed, "lat", [(place, (place - offset) % lat_count) for place in range(lat_count)]
        )
        for offset in OFFSETS
    ]
    (packed,) = call(axial_project_kernel, [((chips, 3 * slots, PAIR), bf16)], [VMEM] * 3)(
        normed, peer, weights
    )
    row_head = lax.all_to_all(packed, "lon", 0, 0, axis_index_groups=groups, tiled=True)
    (band,) = call(
        functools.partial(band_kernel, lat_count, lon_count),
        [((tokens, band_width), bf16)],
        [SMEM, SMEM] + [VMEM] * 5 + [HBM] * 3,
        [
            pltpu.VMEM((pairs, width, PAIR), bf16),
            pltpu.VMEM((pairs, width, 2 * PAIR), bf16),
            pltpu.SemaphoreType.DMA((pairs, 3)),
        ],
        BAND_FLOPS,
    )(row_points, band_mask.T, normed, *near, *in_hbm(w_query, w_key, w_value))
    (axial,) = call(
        functools.partial(axial_kernel, lon_count),
        [((chips, slots, PAIR), bf16)],
        [SMEM, VMEM, ANY],
    )(row_points, row_head, band)
    mine = lax.all_to_all(axial, "lon", 0, 0, axis_index_groups=groups, tiled=True)
    other = lax.ppermute(mine, "lon", swap)
    summed, axial_w = call(
        band_out_kernel,
        [((tokens, width), f32), ((axial_width, width), bf16)],
        [HBM, VMEM, HBM],
        [
            pltpu.VMEM((rows, slots, width), f32),
            pltpu.VMEM((band_width, width), bf16),
            pltpu.SemaphoreType.DMA((3,)),
        ],
        BAND_OUT_FLOPS,
    )(*in_hbm(fields), band, *in_hbm(w_out))
    (out,) = call(
        functools.partial(finish_kernel, lon_count),
        [((rows, slots, width), f32)],
        [SMEM] + [VMEM] * 4,
    )(row_points, summed, mine, other, axial_w)
    return out


def solution(mesh):
    in_specs = (P("lat", "lon", None), P(), P(), P(), P(), P(), P(), P())
    out_specs = P("lat", "lon", None)
    return jax.shard_map(
        on_device, mesh=mesh, in_specs=in_specs, out_specs=out_specs, check_vma=False
    )
```

```python
import functools

import jax
import jax.numpy as jnp
from jax import lax
from jax.experimental import pallas as pl
from jax.experimental.pallas import tpu as pltpu
from jax.sharding import PartitionSpec as P

HEADS = 16
HEAD_DIM = 64
AXIAL_HEADS = 8
REACH = 2
EPS = 1e-05
DEAD = -1e30
PAIR = 2 * HEAD_DIM
SCALE = HEAD_DIM**-0.5
OFFSETS = (-2, -1, 1, 2)
BAND_FLOPS = 20_000_000_000
BAND_OUT_FLOPS = 20_000_000_000

VMEM = pl.BlockSpec(memory_space=pltpu.VMEM)
SMEM = pl.BlockSpec(memory_space=pltpu.SMEM)
HBM = pl.BlockSpec(memory_space=pltpu.HBM)
ANY = pl.BlockSpec(memory_space=pl.ANY)


def dot(a, b):
    return jnp.dot(a, b, preferred_element_type=jnp.float32)


def dot_t(a, b):
    return lax.dot_general(a, b, (((1,), (1,)), ((), ())), preferred_element_type=jnp.float32)


def half_roll(value):
    return pltpu.roll(value, HEAD_DIM, 1)


def low_half(shape):
    return lax.broadcasted_iota(jnp.int32, shape, 1) < HEAD_DIM


def live_count(points, tile, tiles):
    return points // tiles + (tile < points % tiles).astype(jnp.int32)


def norm_kernel(
    fields_hbm, gain_hbm, wq_hbm, wk_hbm, wv_hbm, out_ref, weights_ref, fields_ref, gain_ref, sems
):
    core = lax.rem(lax.axis_index("lon"), 2)
    width = weights_ref.shape[2]
    columns = pl.ds(pl.multiple_of(core * width, width), width)
    rows = fields_hbm.shape[0]
    slots = fields_hbm.shape[1]
    gain_copy = pltpu.make_async_copy(gain_hbm, gain_ref, sems.at[0])
    row_copies = [
        pltpu.make_async_copy(fields_hbm.at[row], fields_ref.at[row], sems.at[1 + row])
        for row in range(rows)
    ]
    rest = [
        pltpu.make_async_copy(hbm.at[:, columns], weights_ref.at[place], sems.at[1 + rows + place])
        for place, hbm in enumerate((wq_hbm, wk_hbm, wv_hbm))
    ]
    for copy in [gain_copy] + row_copies + rest:
        copy.start()
    gain_copy.wait()
    for row in range(rows):
        row_copies[row].wait()
        values = fields_ref[row]
        mean = jnp.mean(values, axis=-1, keepdims=True)
        centred = values - mean
        var = jnp.mean(centred * centred, axis=-1, keepdims=True)
        out_ref[row * slots : (row + 1) * slots, :] = (
            centred * lax.rsqrt(var + EPS) * gain_ref[...]
        ).astype(jnp.bfloat16)
    for copy in rest:
        copy.wait()


def axial_project_kernel(own_ref, peer_ref, weights_ref, out_hbm, out_ref, sems):
    tokens = own_ref.shape[0]
    items, third, _ = out_ref.shape
    slots = third // 3
    rows = tokens // slots
    heads = AXIAL_HEADS // 2
    both = jnp.concatenate([own_ref[...], peer_ref[...]], axis=0)
    low = low_half((tokens, PAIR))
    copies = []
    for part in range(3):
        result = dot(both, weights_ref[part])
        if part == 0:
            result = result.astype(jnp.bfloat16).astype(jnp.float32) * SCALE
        for pair in range(heads // 2):
            span = slice(pair * PAIR, (pair + 1) * PAIR)
            own, peer = result[:tokens, span], result[tokens:, span]
            sides = (
                jnp.where(low, own, half_roll(peer)),
                jnp.where(low, half_roll(own), peer),
            )
            for side in range(2):
                packed = sides[side].astype(jnp.bfloat16)
                for row in range(rows):
                    out_ref[row * heads + pair * 2 + side, part * slots : (part + 1) * slots, :] = (
                        packed[row * slots : (row + 1) * slots]
                    )
        block = pl.ds(part * slots, slots)
        copies.append(
            pltpu.make_async_copy(out_ref.at[:, block], out_hbm.at[:, block], sems.at[part])
        )
        copies[part].start()
    for copy in copies:
        copy.wait()


def axial_kernel(lon_count, points_ref, in_ref, after_ref, out_ref):
    lon = lax.axis_index("lon")
    core = lax.rem(lon, 2)
    chip = lon // 2
    chips, third, _ = in_ref.shape
    slots = third // 3
    heads = AXIAL_HEADS // 2
    tokens = chips * slots
    points = points_ref[lax.axis_index("lat") * (chips // heads) + chip // heads]
    slot = lax.broadcasted_iota(jnp.int32, (slots, PAIR), 0)

    def bias_of(which):
        return jnp.concatenate(
            [
                jnp.where(slot < live_count(points, 2 * place + which, lon_count), 0.0, DEAD)
                for place in range(chips)
            ],
            axis=0,
        )

    lane = lax.broadcasted_iota(jnp.int32, (tokens, PAIR), 1)
    low = lane < HEAD_DIM
    first_lane = (lane == 0).astype(jnp.float32)
    high_lane = (lane == HEAD_DIM).astype(jnp.float32)

    def part(index):
        return in_ref[:, index * slots : (index + 1) * slots, :].reshape(tokens, PAIR)

    bf16 = jnp.bfloat16
    query = part(0).astype(jnp.float32)
    key = part(1).astype(jnp.float32)
    value = part(2)
    key_own = jnp.where(low, key, high_lane * bias_of(core)).astype(bf16)
    key_peer = jnp.where(low, first_lane * bias_of(1 - core), key).astype(bf16)
    rolled = half_roll(query)
    value_rolled = half_roll(value.astype(jnp.float32)).astype(bf16)
    plain = jnp.concatenate([value, value_rolled], axis=0)
    crossed = jnp.concatenate([value_rolled, value], axis=0)
    blocks = (
        (jnp.where(low, query, high_lane), jnp.where(low, first_lane, rolled), plain),
        (jnp.where(low, rolled, high_lane), jnp.where(low, first_lane, query), crossed),
    )
    outs = []
    for for_own, for_peer, values in blocks:
        scores = jnp.concatenate(
            [dot_t(for_own.astype(bf16), key_own), dot_t(for_peer.astype(bf16), key_peer)], axis=1
        )
        weights = jnp.exp(scores - jnp.max(scores, axis=-1, keepdims=True))
        total = jnp.sum(weights, axis=-1, keepdims=True)
        outs.append(dot(weights.astype(bf16), values) / total)
    out_ref[...] = jnp.where(low, outs[0], outs[1]).astype(bf16).reshape(chips, slots, PAIR)


def band_kernel(
    lat_count, lon_count, points_ref, mask_ref, own_ref, m2_ref, m1_ref, p1_ref, p2_ref,
    wq_hbm, wk_hbm, wv_hbm, out_ref, wq_ref, wkv_ref, sems,
):
    pairs = (HEADS - AXIAL_HEADS) // 2
    first = AXIAL_HEADS * HEAD_DIM
    copies = []
    for pair in range(pairs):
        columns = pl.ds(first + pair * PAIR, PAIR)
        copies.append(
            [
                pltpu.make_async_copy(wk_hbm.at[:, columns], wkv_ref.at[pair, :, pl.ds(0, PAIR)], sems.at[pair, 0]),
                pltpu.make_async_copy(wv_hbm.at[:, columns], wkv_ref.at[pair, :, pl.ds(PAIR, PAIR)], sems.at[pair, 1]),
                pltpu.make_async_copy(wq_hbm.at[:, columns], wq_ref.at[pair], sems.at[pair, 2]),
            ]
        )
    for group in copies:
        for copy in group:
            copy.start()
    lat = lax.axis_index("lat")
    lon = lax.axis_index("lon")
    tokens = own_ref.shape[0]
    slots = 32
    rows = tokens // slots
    bands = (0,) + OFFSETS
    own = own_ref[...]
    everything = jnp.concatenate([own, m2_ref[...], m1_ref[...], p1_ref[...], p2_ref[...]], axis=0)
    keys = everything.shape[0]
    slot = lax.broadcasted_iota(jnp.int32, (slots, PAIR), 0)
    blocks = []
    for offset in bands:
        source = lat + offset
        held = jnp.clip(source, 0, lat_count - 1)
        if offset == 0:
            allowed = jnp.int32(1)
        else:
            column = offset + REACH if offset < 0 else offset + REACH - 1
            inside = (source >= 0) & (source < lat_count)
            allowed = jnp.where(inside & (mask_ref[column, lat] == 1), 1, 0)
        for row in range(rows):
            count = live_count(points_ref[held * rows + row], lon, lon_count) * allowed
            blocks.append(jnp.where(slot < count, 0.0, DEAD))
    bias = jnp.concatenate(blocks, axis=0).astype(jnp.bfloat16)
    lane_k = lax.broadcasted_iota(jnp.int32, (keys, PAIR), 1)
    lane_q = lax.broadcasted_iota(jnp.int32, (tokens, PAIR), 1)
    zero_k = jnp.zeros((keys, PAIR), jnp.bfloat16)
    low_o = lane_q < HEAD_DIM
    for pair in range(pairs):
        for copy in copies[pair]:
            copy.wait()
        kv = dot(everything, wkv_ref[pair]).astype(jnp.bfloat16)
        k, v = kv[:, :PAIR], kv[:, PAIR:]
        q = dot(own, wq_ref[pair]).astype(jnp.bfloat16) * jnp.bfloat16(SCALE)
        outs = []
        for side in range(2):
            spare = HEAD_DIM if side == 0 else 0
            mine_q = (lane_q < HEAD_DIM) if side == 0 else (lane_q >= HEAD_DIM)
            mine_k = (lane_k < HEAD_DIM) if side == 0 else (lane_k >= HEAD_DIM)
            q_side = jnp.where(mine_q, q, (lane_q == spare).astype(jnp.bfloat16))
            k_side = jnp.where(mine_k, k, jnp.where(lane_k == spare, bias, zero_k))
            scores = dot_t(q_side, k_side)
            peak = jnp.max(scores, axis=-1, keepdims=True)
            weights = jnp.exp(scores - peak)
            total = jnp.sum(weights, axis=-1, keepdims=True)
            outs.append(dot(weights.astype(jnp.bfloat16), v) / total)
        out_ref[:, pair * PAIR : (pair + 1) * PAIR] = jnp.where(low_o, outs[0], outs[1]).astype(
            jnp.bfloat16
        )


def band_out_kernel(fields_hbm, band_ref, w_hbm, out_ref, axial_w_ref, fields_ref, w_ref, sems):
    core = lax.rem(lax.axis_index("lon"), 2)
    rows, slots, width = fields_ref.shape
    depth = w_ref.shape[0]
    heads = AXIAL_HEADS // 2
    first = [
        pltpu.make_async_copy(w_hbm.at[pl.ds(depth, depth)], w_ref, sems.at[0]),
        pltpu.make_async_copy(fields_hbm, fields_ref, sems.at[1]),
    ]
    rest = []
    for head in range(heads):
        for side in range(2):
            source = (jnp.where(side == 0, core, 1 - core) * heads + head) * HEAD_DIM
            rest.append(
                pltpu.make_async_copy(
                    w_hbm.at[pl.ds(pl.multiple_of(source, HEAD_DIM), HEAD_DIM)],
                    axial_w_ref.at[pl.ds(head * PAIR + side * HEAD_DIM, HEAD_DIM)],
                    sems.at[2 + head * 2 + side],
                )
            )
    for copy in first + rest:
        copy.start()
    for copy in first:
        copy.wait()
    out_ref[...] = fields_ref[...].reshape(rows * slots, width) + dot(band_ref[...], w_ref[...])
    for copy in rest:
        copy.wait()


def finish_kernel(lon_count, points_ref, sum_ref, mine_ref, other_ref, w_ref, out_hbm, out_ref, sems):
    lon = lax.axis_index("lon")
    lat = lax.axis_index("lat")
    rows, slots, width = out_ref.shape
    heads = AXIAL_HEADS // 2
    low = low_half((slots, PAIR))
    mixed = jnp.concatenate(
        [
            jnp.concatenate(
                [
                    jnp.where(low, mine_ref[row * heads + head], other_ref[row * heads + head])
                    for head in range(heads)
                ],
                axis=1,
            )
            for row in range(rows)
        ],
        axis=0,
    )
    step = 256
    slot = lax.broadcasted_iota(jnp.int32, (slots, step), 0)
    counts = [live_count(points_ref[lat * rows + row], lon, lon_count) for row in range(rows)]
    copies = []
    for place in range(width // step):
        span = pl.ds(place * step, step)
        result = sum_ref[:, span] + dot(mixed, w_ref[:, span])
        for row in range(rows):
            out_ref[row, :, span] = jnp.where(
                slot < counts[row], result[row * slots : (row + 1) * slots], 0.0
            )
        copies.append(
            pltpu.make_async_copy(out_ref.at[:, :, span], out_hbm.at[:, :, span], sems.at[place])
        )
        copies[place].start()
    for copy in copies:
        copy.wait()


def call(kernel, shapes, specs, scratch=(), flops=0, out=VMEM):
    return pl.pallas_call(
        kernel,
        out_shape=[jax.ShapeDtypeStruct(shape, dtype) for shape, dtype in shapes],
        in_specs=specs,
        out_specs=[out] * len(shapes),
        scratch_shapes=scratch,
        compiler_params=pltpu.CompilerParams(vmem_limit_bytes=24 * 1024 * 1024),
        cost_estimate=pl.CostEstimate(flops=flops, transcendentals=0, bytes_accessed=0) if flops else None,
    )


def on_device(fields, row_points, band_mask, norm_gain, w_query, w_key, w_value, w_out):
    rows, slots, width = fields.shape
    lat_count = lax.axis_size("lat")
    lon_count = lax.axis_size("lon")
    tokens = rows * slots
    chips = lon_count // 2
    axial_width = AXIAL_HEADS * HEAD_DIM
    band_width = (HEADS - AXIAL_HEADS) * HEAD_DIM
    pairs = band_width // PAIR
    bf16, f32 = jnp.bfloat16, jnp.float32
    groups = [[2 * chip + core for chip in range(chips)] for core in range(2)]
    swap = [(place, place + 1 - 2 * (place % 2)) for place in range(lon_count)]

    def in_hbm(*arrays):
        return [pltpu.with_memory_space_constraint(array, pltpu.HBM) for array in arrays]

    normed, weights = call(
        norm_kernel,
        [((tokens, width), bf16), ((3, width, axial_width // 2), bf16)],
        [HBM] * 5,
        [
            pltpu.VMEM((rows, slots, width), f32),
            pltpu.VMEM((1, width), f32),
            pltpu.SemaphoreType.DMA((4 + rows,)),
        ],
    )(*in_hbm(fields, norm_gain.reshape(1, width), w_query, w_key, w_value))
    peer = lax.ppermute(normed, "lon", swap)
    near = [
        lax.ppermute(
            normed, "lat", [(place, (place - offset) % lat_count) for place in range(lat_count)]
        )
        for offset in OFFSETS
    ]
    (packed,) = call(
        axial_project_kernel,
        [((chips, 3 * slots, PAIR), bf16)],
        [VMEM] * 3,
        [pltpu.VMEM((chips, 3 * slots, PAIR), bf16), pltpu.SemaphoreType.DMA((3,))],
        out=ANY,
    )(normed, peer, weights)
    row_head = lax.all_to_all(packed, "lon", 0, 0, axis_index_groups=groups, tiled=True)
    (band,) = call(
        functools.partial(band_kernel, lat_count, lon_count),
        [((tokens, band_width), bf16)],
        [SMEM, SMEM] + [VMEM] * 5 + [HBM] * 3,
        [
            pltpu.VMEM((pairs, width, PAIR), bf16),
            pltpu.VMEM((pairs, width, 2 * PAIR), bf16),
            pltpu.SemaphoreType.DMA((pairs, 3)),
        ],
        BAND_FLOPS,
    )(row_points, band_mask.T, normed, *near, *in_hbm(w_query, w_key, w_value))
    summed, axial_w = call(
        band_out_kernel,
        [((tokens, width), f32), ((axial_width, width), bf16)],
        [HBM, VMEM, HBM],
        [
            pltpu.VMEM((rows, slots, width), f32),
            pltpu.VMEM((band_width, width), bf16),
            pltpu.SemaphoreType.DMA((2 + AXIAL_HEADS,)),
        ],
        BAND_OUT_FLOPS,
    )(*in_hbm(fields), band, *in_hbm(w_out))
    (axial,) = call(
        functools.partial(axial_kernel, lon_count),
        [((chips, slots, PAIR), bf16)],
        [SMEM, VMEM, ANY],
    )(row_points, row_head, summed)
    mine = lax.all_to_all(axial, "lon", 0, 0, axis_index_groups=groups, tiled=True)
    other = lax.ppermute(mine, "lon", swap)
    (out,) = call(
        functools.partial(finish_kernel, lon_count),
        [((rows, slots, width), f32)],
        [SMEM] + [VMEM] * 4,
        [pltpu.VMEM((rows, slots, width), f32), pltpu.SemaphoreType.DMA((4,))],
        out=ANY,
    )(row_points, summed, mine, other, axial_w)
    return out


def solution(mesh):
    in_specs = (P("lat", "lon", None), P(), P(), P(), P(), P(), P(), P())
    out_specs = P("lat", "lon", None)
    return jax.shard_map(
        on_device, mesh=mesh, in_specs=in_specs, out_specs=out_specs, check_vma=False
    )
```

```python
import functools

import jax
import jax.numpy as jnp
from jax import lax
from jax.experimental import pallas as pl
from jax.experimental.pallas import tpu as pltpu
from jax.sharding import PartitionSpec as P

HEADS = 16
HEAD_DIM = 64
AXIAL_HEADS = 8
REACH = 2
EPS = 1e-05
DEAD = -1e30
PAIR = 2 * HEAD_DIM
SCALE = HEAD_DIM**-0.5
OFFSETS = (-2, -1, 1, 2)
BAND_FLOPS = 20_000_000_000
BAND_OUT_FLOPS = 20_000_000_000

VMEM = pl.BlockSpec(memory_space=pltpu.VMEM)
SMEM = pl.BlockSpec(memory_space=pltpu.SMEM)
HBM = pl.BlockSpec(memory_space=pltpu.HBM)
ANY = pl.BlockSpec(memory_space=pl.ANY)


def dot(a, b):
    return jnp.dot(a, b, preferred_element_type=jnp.float32)


def dot_t(a, b):
    return lax.dot_general(a, b, (((1,), (1,)), ((), ())), preferred_element_type=jnp.float32)


def half_roll(value):
    return pltpu.roll(value, HEAD_DIM, 1)


def low_half(shape):
    return lax.broadcasted_iota(jnp.int32, shape, 1) < HEAD_DIM


def live_count(points, tile, tiles):
    return points // tiles + (tile < points % tiles).astype(jnp.int32)


def norm_kernel(
    fields_hbm, gain_hbm, wq_hbm, wk_hbm, wv_hbm, out_ref, weights_ref, fields_ref, gain_ref, sems
):
    core = lax.rem(lax.axis_index("lon"), 2)
    width = weights_ref.shape[2]
    columns = pl.ds(pl.multiple_of(core * width, width), width)
    rows = fields_hbm.shape[0]
    slots = fields_hbm.shape[1]
    gain_copy = pltpu.make_async_copy(gain_hbm, gain_ref, sems.at[0])
    row_copies = [
        pltpu.make_async_copy(fields_hbm.at[row], fields_ref.at[row], sems.at[1 + row])
        for row in range(rows)
    ]
    rest = [
        pltpu.make_async_copy(hbm.at[:, columns], weights_ref.at[place], sems.at[1 + rows + place])
        for place, hbm in enumerate((wq_hbm, wk_hbm, wv_hbm))
    ]
    for copy in [gain_copy] + row_copies + rest:
        copy.start()
    gain_copy.wait()
    for row in range(rows):
        row_copies[row].wait()
        values = fields_ref[row]
        mean = jnp.mean(values, axis=-1, keepdims=True)
        centred = values - mean
        var = jnp.mean(centred * centred, axis=-1, keepdims=True)
        out_ref[row * slots : (row + 1) * slots, :] = (
            centred * lax.rsqrt(var + EPS) * gain_ref[...]
        ).astype(jnp.bfloat16)
    for copy in rest:
        copy.wait()


def axial_project_kernel(own_ref, peer_ref, weights_ref, out_hbm, out_ref, sems):
    tokens = own_ref.shape[0]
    items, third, _ = out_ref.shape
    slots = third // 3
    rows = tokens // slots
    heads = AXIAL_HEADS // 2
    both = jnp.concatenate([own_ref[...], peer_ref[...]], axis=0)
    low = low_half((tokens, PAIR))
    copies = []
    for part in range(3):
        result = dot(both, weights_ref[part])
        if part == 0:
            result = result.astype(jnp.bfloat16).astype(jnp.float32) * SCALE
        for pair in range(heads // 2):
            span = slice(pair * PAIR, (pair + 1) * PAIR)
            own, peer = result[:tokens, span], result[tokens:, span]
            sides = (
                jnp.where(low, own, half_roll(peer)),
                jnp.where(low, half_roll(own), peer),
            )
            for side in range(2):
                packed = sides[side].astype(jnp.bfloat16)
                for row in range(rows):
                    out_ref[row * heads + pair * 2 + side, part * slots : (part + 1) * slots, :] = (
                        packed[row * slots : (row + 1) * slots]
                    )
        block = pl.ds(part * slots, slots)
        copies.append(
            pltpu.make_async_copy(out_ref.at[:, block], out_hbm.at[:, block], sems.at[part])
        )
        copies[part].start()
    for copy in copies:
        copy.wait()


def axial_kernel(lon_count, points_ref, in_ref, after_ref, out_ref):
    lon = lax.axis_index("lon")
    core = lax.rem(lon, 2)
    chip = lon // 2
    chips, third, _ = in_ref.shape
    slots = third // 3
    heads = AXIAL_HEADS // 2
    tokens = chips * slots
    points = points_ref[lax.axis_index("lat") * (chips // heads) + chip // heads]
    slot = lax.broadcasted_iota(jnp.int32, (slots, PAIR), 0)

    def bias_of(which):
        return jnp.concatenate(
            [
                jnp.where(slot < live_count(points, 2 * place + which, lon_count), 0.0, DEAD)
                for place in range(chips)
            ],
            axis=0,
        )

    lane = lax.broadcasted_iota(jnp.int32, (tokens, PAIR), 1)
    low = lane < HEAD_DIM
    first_lane = (lane == 0).astype(jnp.float32)
    high_lane = (lane == HEAD_DIM).astype(jnp.float32)

    def part(index):
        return in_ref[:, index * slots : (index + 1) * slots, :].reshape(tokens, PAIR)

    bf16 = jnp.bfloat16
    query = part(0).astype(jnp.float32)
    key = part(1).astype(jnp.float32)
    value = part(2)
    key_own = jnp.where(low, key, high_lane * bias_of(core)).astype(bf16)
    key_peer = jnp.where(low, first_lane * bias_of(1 - core), key).astype(bf16)
    rolled = half_roll(query)
    value_rolled = half_roll(value.astype(jnp.float32)).astype(bf16)
    plain = jnp.concatenate([value, value_rolled], axis=0)
    crossed = jnp.concatenate([value_rolled, value], axis=0)
    blocks = (
        (jnp.where(low, query, high_lane), jnp.where(low, first_lane, rolled), plain),
        (jnp.where(low, rolled, high_lane), jnp.where(low, first_lane, query), crossed),
    )
    outs = []
    for for_own, for_peer, values in blocks:
        scores = jnp.concatenate(
            [dot_t(for_own.astype(bf16), key_own), dot_t(for_peer.astype(bf16), key_peer)], axis=1
        )
        weights = jnp.exp(scores - jnp.max(scores, axis=-1, keepdims=True))
        total = jnp.sum(weights, axis=-1, keepdims=True)
        outs.append(dot(weights.astype(bf16), values) / total)
    out_ref[...] = jnp.where(low, outs[0], outs[1]).astype(bf16).reshape(chips, slots, PAIR)


def band_kernel(
    lat_count, lon_count, points_ref, mask_ref, own_ref, m2_ref, m1_ref, p1_ref, p2_ref,
    wq_hbm, wk_hbm, wv_hbm, out_ref, weights_ref, sems,
):
    first = AXIAL_HEADS * HEAD_DIM
    columns = pl.ds(first, weights_ref.shape[2])
    copies = [
        pltpu.make_async_copy(hbm.at[:, columns], weights_ref.at[place], sems.at[place])
        for place, hbm in enumerate((wk_hbm, wv_hbm, wq_hbm))
    ]
    for copy in copies:
        copy.start()
    lat = lax.axis_index("lat")
    lon = lax.axis_index("lon")
    tokens = own_ref.shape[0]
    slots = 32
    rows = tokens // slots
    bf16 = jnp.bfloat16
    own = own_ref[...]
    everything = jnp.concatenate([own, m2_ref[...], m1_ref[...], p1_ref[...], p2_ref[...]], axis=0)
    keys = everything.shape[0]
    slot = lax.broadcasted_iota(jnp.int32, (slots, PAIR), 0)
    blocks = []
    for offset in (0,) + OFFSETS:
        source = lat + offset
        held = jnp.clip(source, 0, lat_count - 1)
        if offset == 0:
            allowed = jnp.int32(1)
        else:
            column = offset + REACH if offset < 0 else offset + REACH - 1
            inside = (source >= 0) & (source < lat_count)
            allowed = jnp.where(inside & (mask_ref[column, lat] == 1), 1, 0)
        for row in range(rows):
            count = live_count(points_ref[held * rows + row], lon, lon_count) * allowed
            blocks.append(jnp.where(slot < count, 0.0, DEAD))
    bias = jnp.concatenate(blocks, axis=0)
    lane_k = lax.broadcasted_iota(jnp.int32, (keys, PAIR), 1)
    lane_q = lax.broadcasted_iota(jnp.int32, (tokens, PAIR), 1)
    low_k, low_q = lane_k < HEAD_DIM, lane_q < HEAD_DIM
    bias_high = jnp.where(lane_k == HEAD_DIM, bias, 0.0).astype(bf16)
    bias_low = jnp.where(lane_k == 0, bias, 0.0).astype(bf16)
    one_high = (lane_q == HEAD_DIM).astype(bf16)
    one_low = (lane_q == 0).astype(bf16)
    copies[0].wait()
    key = dot(everything, weights_ref[0]).astype(bf16)
    copies[1].wait()
    value = dot(everything, weights_ref[1]).astype(bf16)
    copies[2].wait()
    query = dot(own, weights_ref[2]).astype(bf16) * bf16(SCALE)
    for pair in range((HEADS - AXIAL_HEADS) // 2):
        span = slice(pair * PAIR, (pair + 1) * PAIR)
        q, k, v = query[:, span], key[:, span], value[:, span]
        scores = jnp.concatenate(
            [
                dot_t(jnp.where(low_q, q, one_high), jnp.where(low_k, k, bias_high)),
                dot_t(jnp.where(low_q, one_low, q), jnp.where(low_k, bias_low, k)),
            ],
            axis=0,
        )
        weights = jnp.exp(scores - jnp.max(scores, axis=-1, keepdims=True))
        total = jnp.sum(weights, axis=-1, keepdims=True)
        mixed = dot(weights.astype(bf16), v) / total
        out_ref[:, span] = jnp.where(low_q, mixed[:tokens], mixed[tokens:]).astype(bf16)


def band_out_kernel(fields_hbm, band_ref, w_hbm, out_ref, axial_w_ref, fields_ref, w_ref, sems):
    core = lax.rem(lax.axis_index("lon"), 2)
    rows, slots, width = fields_ref.shape
    depth = w_ref.shape[0]
    heads = AXIAL_HEADS // 2
    first = [
        pltpu.make_async_copy(w_hbm.at[pl.ds(depth, depth)], w_ref, sems.at[0]),
        pltpu.make_async_copy(fields_hbm, fields_ref, sems.at[1]),
    ]
    rest = []
    for head in range(heads):
        for side in range(2):
            source = (jnp.where(side == 0, core, 1 - core) * heads + head) * HEAD_DIM
            rest.append(
                pltpu.make_async_copy(
                    w_hbm.at[pl.ds(pl.multiple_of(source, HEAD_DIM), HEAD_DIM)],
                    axial_w_ref.at[pl.ds(head * PAIR + side * HEAD_DIM, HEAD_DIM)],
                    sems.at[2 + head * 2 + side],
                )
            )
    for copy in first + rest:
        copy.start()
    for copy in first:
        copy.wait()
    out_ref[...] = fields_ref[...].reshape(rows * slots, width) + dot(band_ref[...], w_ref[...])
    for copy in rest:
        copy.wait()


def finish_kernel(lon_count, points_ref, sum_ref, mine_ref, other_ref, w_ref, out_hbm, out_ref, sems):
    lon = lax.axis_index("lon")
    lat = lax.axis_index("lat")
    rows, slots, width = out_ref.shape
    heads = AXIAL_HEADS // 2
    low = low_half((slots, PAIR))
    mixed = jnp.concatenate(
        [
            jnp.concatenate(
                [
                    jnp.where(low, mine_ref[row * heads + head], other_ref[row * heads + head])
                    for head in range(heads)
                ],
                axis=1,
            )
            for row in range(rows)
        ],
        axis=0,
    )
    step = 256
    slot = lax.broadcasted_iota(jnp.int32, (slots, step), 0)
    counts = [live_count(points_ref[lat * rows + row], lon, lon_count) for row in range(rows)]
    copies = []
    for place in range(width // step):
        span = pl.ds(place * step, step)
        result = sum_ref[:, span] + dot(mixed, w_ref[:, span])
        for row in range(rows):
            out_ref[row, :, span] = jnp.where(
                slot < counts[row], result[row * slots : (row + 1) * slots], 0.0
            )
        copies.append(
            pltpu.make_async_copy(out_ref.at[:, :, span], out_hbm.at[:, :, span], sems.at[place])
        )
        copies[place].start()
    for copy in copies:
        copy.wait()


def call(kernel, shapes, specs, scratch=(), flops=0, out=VMEM):
    return pl.pallas_call(
        kernel,
        out_shape=[jax.ShapeDtypeStruct(shape, dtype) for shape, dtype in shapes],
        in_specs=specs,
        out_specs=[out] * len(shapes),
        scratch_shapes=scratch,
        compiler_params=pltpu.CompilerParams(vmem_limit_bytes=24 * 1024 * 1024),
        cost_estimate=pl.CostEstimate(flops=flops, transcendentals=0, bytes_accessed=0) if flops else None,
    )


def on_device(fields, row_points, band_mask, norm_gain, w_query, w_key, w_value, w_out):
    rows, slots, width = fields.shape
    lat_count = lax.axis_size("lat")
    lon_count = lax.axis_size("lon")
    tokens = rows * slots
    chips = lon_count // 2
    axial_width = AXIAL_HEADS * HEAD_DIM
    band_width = (HEADS - AXIAL_HEADS) * HEAD_DIM
    bf16, f32 = jnp.bfloat16, jnp.float32
    groups = [[2 * chip + core for chip in range(chips)] for core in range(2)]
    swap = [(place, place + 1 - 2 * (place % 2)) for place in range(lon_count)]

    def in_hbm(*arrays):
        return [pltpu.with_memory_space_constraint(array, pltpu.HBM) for array in arrays]

    normed, weights = call(
        norm_kernel,
        [((tokens, width), bf16), ((3, width, axial_width // 2), bf16)],
        [HBM] * 5,
        [
            pltpu.VMEM((rows, slots, width), f32),
            pltpu.VMEM((1, width), f32),
            pltpu.SemaphoreType.DMA((4 + rows,)),
        ],
    )(*in_hbm(fields, norm_gain.reshape(1, width), w_query, w_key, w_value))
    peer = lax.ppermute(normed, "lon", swap)
    near = [
        lax.ppermute(
            normed, "lat", [(place, (place - offset) % lat_count) for place in range(lat_count)]
        )
        for offset in OFFSETS
    ]
    (packed,) = call(
        axial_project_kernel,
        [((chips, 3 * slots, PAIR), bf16)],
        [VMEM] * 3,
        [pltpu.VMEM((chips, 3 * slots, PAIR), bf16), pltpu.SemaphoreType.DMA((3,))],
        out=ANY,
    )(normed, peer, weights)
    row_head = lax.all_to_all(packed, "lon", 0, 0, axis_index_groups=groups, tiled=True)
    (band,) = call(
        functools.partial(band_kernel, lat_count, lon_count),
        [((tokens, band_width), bf16)],
        [SMEM, SMEM] + [VMEM] * 5 + [HBM] * 3,
        [
            pltpu.VMEM((3, width, band_width), bf16),
            pltpu.SemaphoreType.DMA((3,)),
        ],
        BAND_FLOPS,
    )(row_points, band_mask.T, normed, *near, *in_hbm(w_query, w_key, w_value))
    summed, axial_w = call(
        band_out_kernel,
        [((tokens, width), f32), ((axial_width, width), bf16)],
        [HBM, VMEM, HBM],
        [
            pltpu.VMEM((rows, slots, width), f32),
            pltpu.VMEM((band_width, width), bf16),
            pltpu.SemaphoreType.DMA((2 + AXIAL_HEADS,)),
        ],
        BAND_OUT_FLOPS,
    )(*in_hbm(fields), band, *in_hbm(w_out))
    (axial,) = call(
        functools.partial(axial_kernel, lon_count),
        [((chips, slots, PAIR), bf16)],
        [SMEM, VMEM, ANY],
    )(row_points, row_head, summed)
    mine = lax.all_to_all(axial, "lon", 0, 0, axis_index_groups=groups, tiled=True)
    other = lax.ppermute(mine, "lon", swap)
    (out,) = call(
        functools.partial(finish_kernel, lon_count),
        [((rows, slots, width), f32)],
        [SMEM] + [VMEM] * 4,
        [pltpu.VMEM((rows, slots, width), f32), pltpu.SemaphoreType.DMA((4,))],
        out=ANY,
    )(row_points, summed, mine, other, axial_w)
    return out


def solution(mesh):
    in_specs = (P("lat", "lon", None), P(), P(), P(), P(), P(), P(), P())
    out_specs = P("lat", "lon", None)
    return jax.shard_map(
        on_device, mesh=mesh, in_specs=in_specs, out_specs=out_specs, check_vma=False
    )
```

```python
import functools

import jax
import jax.numpy as jnp
from jax import lax
from jax.experimental import pallas as pl
from jax.experimental.pallas import tpu as pltpu
from jax.sharding import PartitionSpec as P

HEADS = 16
HEAD_DIM = 64
AXIAL_HEADS = 8
REACH = 2
EPS = 1e-05
DEAD = -1e30
PAIR = 2 * HEAD_DIM
SCALE = HEAD_DIM**-0.5
OFFSETS = (-2, -1, 1, 2)
AXIAL_FLOPS = 20_000_000_000
BAND_FLOPS = 20_000_000_000
BAND_OUT_FLOPS = 20_000_000_000

VMEM = pl.BlockSpec(memory_space=pltpu.VMEM)
SMEM = pl.BlockSpec(memory_space=pltpu.SMEM)
HBM = pl.BlockSpec(memory_space=pltpu.HBM)
ANY = pl.BlockSpec(memory_space=pl.ANY)


def dot(a, b):
    return jnp.dot(a, b, preferred_element_type=jnp.float32)


def dot_t(a, b):
    return lax.dot_general(a, b, (((1,), (1,)), ((), ())), preferred_element_type=jnp.float32)


def half_roll(value):
    return pltpu.roll(value, HEAD_DIM, 1)


def low_half(shape):
    return lax.broadcasted_iota(jnp.int32, shape, 1) < HEAD_DIM


def live_count(points, tile, tiles):
    return points // tiles + (tile < points % tiles).astype(jnp.int32)


def norm_kernel(
    fields_hbm, gain_hbm, wq_hbm, wk_hbm, wv_hbm, out_ref, weights_ref, fields_ref, gain_ref, sems
):
    core = lax.rem(lax.axis_index("lon"), 2)
    width = weights_ref.shape[2]
    columns = pl.ds(pl.multiple_of(core * width, width), width)
    rows = fields_hbm.shape[0]
    slots = fields_hbm.shape[1]
    gain_copy = pltpu.make_async_copy(gain_hbm, gain_ref, sems.at[0])
    row_copies = [
        pltpu.make_async_copy(fields_hbm.at[row], fields_ref.at[row], sems.at[1 + row])
        for row in range(rows)
    ]
    rest = [
        pltpu.make_async_copy(hbm.at[:, columns], weights_ref.at[place], sems.at[1 + rows + place])
        for place, hbm in enumerate((wq_hbm, wk_hbm, wv_hbm))
    ]
    for copy in [gain_copy] + row_copies + rest:
        copy.start()
    gain_copy.wait()
    for row in range(rows):
        row_copies[row].wait()
        values = fields_ref[row]
        mean = jnp.mean(values, axis=-1, keepdims=True)
        centred = values - mean
        var = jnp.mean(centred * centred, axis=-1, keepdims=True)
        out_ref[row * slots : (row + 1) * slots, :] = (
            centred * lax.rsqrt(var + EPS) * gain_ref[...]
        ).astype(jnp.bfloat16)
    for copy in rest:
        copy.wait()


def axial_project_kernel(own_ref, peer_ref, weights_ref, out_hbm, out_ref, sems):
    tokens = own_ref.shape[0]
    items, third, _ = out_ref.shape
    slots = third // 3
    rows = tokens // slots
    heads = AXIAL_HEADS // 2
    both = jnp.concatenate([own_ref[...], peer_ref[...]], axis=0)
    low = low_half((tokens, PAIR))
    copies = []
    for part in range(3):
        result = dot(both, weights_ref[part])
        if part == 0:
            result = result.astype(jnp.bfloat16).astype(jnp.float32) * SCALE
        for pair in range(heads // 2):
            span = slice(pair * PAIR, (pair + 1) * PAIR)
            own, peer = result[:tokens, span], result[tokens:, span]
            sides = (
                jnp.where(low, own, half_roll(peer)),
                jnp.where(low, half_roll(own), peer),
            )
            for side in range(2):
                packed = sides[side].astype(jnp.bfloat16)
                for row in range(rows):
                    out_ref[row * heads + pair * 2 + side, part * slots : (part + 1) * slots, :] = (
                        packed[row * slots : (row + 1) * slots]
                    )
        block = pl.ds(part * slots, slots)
        copies.append(
            pltpu.make_async_copy(out_ref.at[:, block], out_hbm.at[:, block], sems.at[part])
        )
        copies[part].start()
    for copy in copies:
        copy.wait()


def packed_part(ref, index):
    chips, third, _ = ref.shape
    slots = third // 3
    return ref[:, index * slots : (index + 1) * slots, :].reshape(chips * slots, PAIR)


def attend(for_own, for_peer, key_own, key_peer, values, out_ref):
    scores = jnp.concatenate([dot_t(for_own, key_own), dot_t(for_peer, key_peer)], axis=1)
    weights = jnp.exp(scores - jnp.max(scores, axis=-1, keepdims=True))
    total = jnp.sum(weights, axis=-1, keepdims=True)
    mixed = dot(weights.astype(jnp.bfloat16), values) / total
    out_ref[...] = mixed.astype(jnp.bfloat16).reshape(out_ref.shape)


def lane_masks(tokens):
    lane = lax.broadcasted_iota(jnp.int32, (tokens, PAIR), 1)
    bf16 = jnp.bfloat16
    return lane < HEAD_DIM, (lane == 0).astype(bf16), (lane == HEAD_DIM).astype(bf16)


def axial_peer_kernel(
    in_ref, bias_own_ref, bias_peer_ref, out_ref, key_own_ref, key_peer_ref, values_ref, rolled_ref
):
    tokens = bias_own_ref.shape[0]
    low, low_one, high_one = lane_masks(tokens)
    query, key, value = (packed_part(in_ref, index) for index in range(3))
    key_own_ref[...] = jnp.where(low, key, bias_own_ref[...])
    key_peer_ref[...] = jnp.where(low, bias_peer_ref[...], key)
    query_rolled, value_rolled = half_roll(query), half_roll(value)
    values_ref[:tokens] = value
    values_ref[tokens:] = value_rolled
    rolled_ref[...] = query_rolled
    attend(
        jnp.where(low, query_rolled, high_one),
        jnp.where(low, low_one, query),
        key_own_ref[...],
        key_peer_ref[...],
        jnp.concatenate([value_rolled, value], axis=0),
        out_ref,
    )


def axial_own_kernel(in_ref, key_own_ref, key_peer_ref, values_ref, rolled_ref, out_ref):
    low, low_one, high_one = lane_masks(rolled_ref.shape[0])
    attend(
        jnp.where(low, packed_part(in_ref, 0), high_one),
        jnp.where(low, low_one, rolled_ref[...]),
        key_own_ref[...],
        key_peer_ref[...],
        values_ref[...],
        out_ref,
    )


def join_kernel(low_ref, high_ref, out_ref):
    items, slots, _ = out_ref.shape
    low = low_half((items * slots, PAIR))
    joined = jnp.where(
        low, low_ref[...].reshape(items * slots, PAIR), high_ref[...].reshape(items * slots, PAIR)
    )
    out_ref[...] = joined.reshape(out_ref.shape)


def band_kernel(
    lat_count, lon_count, points_ref, mask_ref, own_ref, m2_ref, m1_ref, p1_ref, p2_ref,
    wq_hbm, wk_hbm, wv_hbm, out_ref, weights_ref, sems,
):
    first = AXIAL_HEADS * HEAD_DIM
    columns = pl.ds(first, weights_ref.shape[2])
    copies = [
        pltpu.make_async_copy(hbm.at[:, columns], weights_ref.at[place], sems.at[place])
        for place, hbm in enumerate((wk_hbm, wv_hbm, wq_hbm))
    ]
    for copy in copies:
        copy.start()
    lat = lax.axis_index("lat")
    lon = lax.axis_index("lon")
    tokens = own_ref.shape[0]
    slots = 32
    rows = tokens // slots
    bf16 = jnp.bfloat16
    own = own_ref[...]
    everything = jnp.concatenate([own, m2_ref[...], m1_ref[...], p1_ref[...], p2_ref[...]], axis=0)
    keys = everything.shape[0]
    slot = lax.broadcasted_iota(jnp.int32, (slots, PAIR), 0)
    blocks = []
    for offset in (0,) + OFFSETS:
        source = lat + offset
        held = jnp.clip(source, 0, lat_count - 1)
        if offset == 0:
            allowed = jnp.int32(1)
        else:
            column = offset + REACH if offset < 0 else offset + REACH - 1
            inside = (source >= 0) & (source < lat_count)
            allowed = jnp.where(inside & (mask_ref[column, lat] == 1), 1, 0)
        for row in range(rows):
            count = live_count(points_ref[held * rows + row], lon, lon_count) * allowed
            blocks.append(jnp.where(slot < count, 0.0, DEAD))
    bias = jnp.concatenate(blocks, axis=0)
    lane_k = lax.broadcasted_iota(jnp.int32, (keys, PAIR), 1)
    lane_q = lax.broadcasted_iota(jnp.int32, (tokens, PAIR), 1)
    low_k, low_q = lane_k < HEAD_DIM, lane_q < HEAD_DIM
    bias_high = jnp.where(lane_k == HEAD_DIM, bias, 0.0).astype(bf16)
    bias_low = jnp.where(lane_k == 0, bias, 0.0).astype(bf16)
    one_high = (lane_q == HEAD_DIM).astype(bf16)
    one_low = (lane_q == 0).astype(bf16)
    copies[0].wait()
    key = dot(everything, weights_ref[0]).astype(bf16)
    copies[1].wait()
    value = dot(everything, weights_ref[1]).astype(bf16)
    copies[2].wait()
    query = dot(own, weights_ref[2]).astype(bf16) * bf16(SCALE)
    for pair in range((HEADS - AXIAL_HEADS) // 2):
        span = slice(pair * PAIR, (pair + 1) * PAIR)
        q, k, v = query[:, span], key[:, span], value[:, span]
        scores = jnp.concatenate(
            [
                dot_t(jnp.where(low_q, q, one_high), jnp.where(low_k, k, bias_high)),
                dot_t(jnp.where(low_q, one_low, q), jnp.where(low_k, bias_low, k)),
            ],
            axis=0,
        )
        weights = jnp.exp(scores - jnp.max(scores, axis=-1, keepdims=True))
        total = jnp.sum(weights, axis=-1, keepdims=True)
        mixed = dot(weights.astype(bf16), v) / total
        out_ref[:, span] = jnp.where(low_q, mixed[:tokens], mixed[tokens:]).astype(bf16)


def band_out_kernel(
    lon_count, points_ref, fields_hbm, band_ref, w_hbm, out_ref, axial_w_ref, bias_own_ref, bias_peer_ref,
    fields_ref, w_ref, sems,
):
    lon = lax.axis_index("lon")
    core = lax.rem(lon, 2)
    chip = lon // 2
    rows, slots, width = fields_ref.shape
    depth = w_ref.shape[0]
    heads = AXIAL_HEADS // 2
    first = [
        pltpu.make_async_copy(w_hbm.at[pl.ds(depth, depth)], w_ref, sems.at[0]),
        pltpu.make_async_copy(fields_hbm, fields_ref, sems.at[1]),
    ]
    rest = []
    for head in range(heads):
        for side in range(2):
            source = (jnp.where(side == 0, core, 1 - core) * heads + head) * HEAD_DIM
            rest.append(
                pltpu.make_async_copy(
                    w_hbm.at[pl.ds(pl.multiple_of(source, HEAD_DIM), HEAD_DIM)],
                    axial_w_ref.at[pl.ds(head * PAIR + side * HEAD_DIM, HEAD_DIM)],
                    sems.at[2 + head * 2 + side],
                )
            )
    for copy in first + rest:
        copy.start()
    points = points_ref[lax.axis_index("lat") * rows + chip // heads]
    slot = lax.broadcasted_iota(jnp.int32, (slots, PAIR), 0)
    lane = lax.broadcasted_iota(jnp.int32, (slots, PAIR), 1)
    for place in range(lon_count // 2):
        part = pl.ds(place * slots, slots)
        dead_own = slot >= live_count(points, 2 * place + core, lon_count)
        dead_peer = slot >= live_count(points, 2 * place + 1 - core, lon_count)
        bias_own_ref[part, :] = jnp.where(dead_own & (lane == HEAD_DIM), DEAD, 0.0).astype(jnp.bfloat16)
        bias_peer_ref[part, :] = jnp.where(dead_peer & (lane == 0), DEAD, 0.0).astype(jnp.bfloat16)
    for copy in first:
        copy.wait()
    out_ref[...] = fields_ref[...].reshape(rows * slots, width) + dot(band_ref[...], w_ref[...])
    for copy in rest:
        copy.wait()


def finish_kernel(lon_count, points_ref, sum_ref, mixed_ref, w_ref, out_hbm, out_ref, sems):
    lon = lax.axis_index("lon")
    lat = lax.axis_index("lat")
    rows, slots, width = out_ref.shape
    heads = AXIAL_HEADS // 2
    mixed = jnp.concatenate(
        [
            jnp.concatenate([mixed_ref[row * heads + head] for head in range(heads)], axis=1)
            for row in range(rows)
        ],
        axis=0,
    )
    step = 256
    slot = lax.broadcasted_iota(jnp.int32, (slots, step), 0)
    counts = [live_count(points_ref[lat * rows + row], lon, lon_count) for row in range(rows)]
    copies = []
    for place in range(width // step):
        span = pl.ds(place * step, step)
        result = sum_ref[:, span] + dot(mixed, w_ref[:, span])
        for row in range(rows):
            out_ref[row, :, span] = jnp.where(
                slot < counts[row], result[row * slots : (row + 1) * slots], 0.0
            )
        copies.append(
            pltpu.make_async_copy(out_ref.at[:, :, span], out_hbm.at[:, :, span], sems.at[place])
        )
        copies[place].start()
    for copy in copies:
        copy.wait()


def call(kernel, shapes, specs, scratch=(), flops=0, out=VMEM):
    return pl.pallas_call(
        kernel,
        out_shape=[jax.ShapeDtypeStruct(shape, dtype) for shape, dtype in shapes],
        in_specs=specs,
        out_specs=[out] * len(shapes),
        scratch_shapes=scratch,
        compiler_params=pltpu.CompilerParams(vmem_limit_bytes=24 * 1024 * 1024),
        cost_estimate=pl.CostEstimate(flops=flops, transcendentals=0, bytes_accessed=0) if flops else None,
    )


def on_device(fields, row_points, band_mask, norm_gain, w_query, w_key, w_value, w_out):
    rows, slots, width = fields.shape
    lat_count = lax.axis_size("lat")
    lon_count = lax.axis_size("lon")
    tokens = rows * slots
    chips = lon_count // 2
    axial_width = AXIAL_HEADS * HEAD_DIM
    band_width = (HEADS - AXIAL_HEADS) * HEAD_DIM
    bf16, f32 = jnp.bfloat16, jnp.float32
    groups = [[2 * chip + core for chip in range(chips)] for core in range(2)]
    swap = [(place, place + 1 - 2 * (place % 2)) for place in range(lon_count)]

    def in_hbm(*arrays):
        return [pltpu.with_memory_space_constraint(array, pltpu.HBM) for array in arrays]

    normed, weights = call(
        norm_kernel,
        [((tokens, width), bf16), ((3, width, axial_width // 2), bf16)],
        [HBM] * 5,
        [
            pltpu.VMEM((rows, slots, width), f32),
            pltpu.VMEM((1, width), f32),
            pltpu.SemaphoreType.DMA((4 + rows,)),
        ],
    )(*in_hbm(fields, norm_gain.reshape(1, width), w_query, w_key, w_value))
    peer = lax.ppermute(normed, "lon", swap)
    near = [
        lax.ppermute(
            normed, "lat", [(place, (place - offset) % lat_count) for place in range(lat_count)]
        )
        for offset in OFFSETS
    ]
    (packed,) = call(
        axial_project_kernel,
        [((chips, 3 * slots, PAIR), bf16)],
        [VMEM] * 3,
        [pltpu.VMEM((chips, 3 * slots, PAIR), bf16), pltpu.SemaphoreType.DMA((3,))],
        out=ANY,
    )(normed, peer, weights)
    row_head = lax.all_to_all(packed, "lon", 0, 0, axis_index_groups=groups, tiled=True)
    (band,) = call(
        functools.partial(band_kernel, lat_count, lon_count),
        [((tokens, band_width), bf16)],
        [SMEM, SMEM] + [VMEM] * 5 + [HBM] * 3,
        [
            pltpu.VMEM((3, width, band_width), bf16),
            pltpu.SemaphoreType.DMA((3,)),
        ],
        BAND_FLOPS,
    )(row_points, band_mask.T, normed, *near, *in_hbm(w_query, w_key, w_value))
    wide = ((chips * slots, PAIR), bf16)
    summed, axial_w, bias_own, bias_peer = call(
        functools.partial(band_out_kernel, lon_count),
        [((tokens, width), f32), ((axial_width, width), bf16), wide, wide],
        [SMEM, HBM, VMEM, HBM],
        [
            pltpu.VMEM((rows, slots, width), f32),
            pltpu.VMEM((band_width, width), bf16),
            pltpu.SemaphoreType.DMA((2 + AXIAL_HEADS,)),
        ],
        BAND_OUT_FLOPS,
    )(row_points, *in_hbm(fields), band, *in_hbm(w_out))
    item = ((chips, slots, PAIR), bf16)
    away, key_own, key_peer, values, rolled = call(
        axial_peer_kernel,
        [item, wide, wide, ((2 * chips * slots, PAIR), bf16), wide],
        [VMEM] * 3,
    )(row_head, bias_own, bias_peer)
    arrived = lax.ppermute(away, "lon", swap)
    (home,) = call(axial_own_kernel, [item], [VMEM] * 5, flops=AXIAL_FLOPS)(
        row_head, key_own, key_peer, values, rolled
    )
    (joined,) = call(join_kernel, [item], [VMEM] * 2)(home, arrived)
    mixed = lax.all_to_all(joined, "lon", 0, 0, axis_index_groups=groups, tiled=True)
    (out,) = call(
        functools.partial(finish_kernel, lon_count),
        [((rows, slots, width), f32)],
        [SMEM] + [VMEM] * 3,
        [pltpu.VMEM((rows, slots, width), f32), pltpu.SemaphoreType.DMA((4,))],
        out=ANY,
    )(row_points, summed, mixed, axial_w)
    return out


def solution(mesh):
    in_specs = (P("lat", "lon", None), P(), P(), P(), P(), P(), P(), P())
    out_specs = P("lat", "lon", None)
    return jax.shard_map(
        on_device, mesh=mesh, in_specs=in_specs, out_specs=out_specs, check_vma=False
    )
```

```python
import functools

import jax
import jax.numpy as jnp
from jax import lax
from jax.experimental import pallas as pl
from jax.experimental.pallas import tpu as pltpu
from jax.sharding import PartitionSpec as P

HEADS = 16
HEAD_DIM = 64
AXIAL_HEADS = 8
REACH = 2
EPS = 1e-05
DEAD = -1e30
PAIR = 2 * HEAD_DIM
SCALE = HEAD_DIM**-0.5
OFFSETS = (-2, -1, 1, 2)
AXIAL_FLOPS = 20_000_000_000
BAND_FLOPS = 20_000_000_000
BAND_OUT_FLOPS = 20_000_000_000

VMEM = pl.BlockSpec(memory_space=pltpu.VMEM)
SMEM = pl.BlockSpec(memory_space=pltpu.SMEM)
HBM = pl.BlockSpec(memory_space=pltpu.HBM)
ANY = pl.BlockSpec(memory_space=pl.ANY)


def dot(a, b):
    return jnp.dot(a, b, preferred_element_type=jnp.float32)


def dot_t(a, b):
    return lax.dot_general(a, b, (((1,), (1,)), ((), ())), preferred_element_type=jnp.float32)


def half_roll(value):
    return pltpu.roll(value, HEAD_DIM, 1)


def low_half(shape):
    return lax.broadcasted_iota(jnp.int32, shape, 1) < HEAD_DIM


def chip_order(chips):
    half = chips // 2
    return [side * half + (z + half // 2) % half for side in range(2) for z in range(half)]


def place_of(chip, chips):
    half = chips // 2
    return chip // half * half + lax.rem(lax.rem(chip, half) + half // 2, half)


def live_count(points, tile, tiles):
    return points // tiles + (tile < points % tiles).astype(jnp.int32)


def norm_kernel(
    fields_hbm, gain_hbm, wq_hbm, wk_hbm, wv_hbm, out_ref, weights_ref, fields_ref, gain_ref, sems
):
    core = lax.rem(lax.axis_index("lon"), 2)
    width = weights_ref.shape[2]
    columns = pl.ds(pl.multiple_of(core * width, width), width)
    rows = fields_hbm.shape[0]
    slots = fields_hbm.shape[1]
    gain_copy = pltpu.make_async_copy(gain_hbm, gain_ref, sems.at[0])
    row_copies = [
        pltpu.make_async_copy(fields_hbm.at[row], fields_ref.at[row], sems.at[1 + row])
        for row in range(rows)
    ]
    rest = [
        pltpu.make_async_copy(hbm.at[:, columns], weights_ref.at[place], sems.at[1 + rows + place])
        for place, hbm in enumerate((wq_hbm, wk_hbm, wv_hbm))
    ]
    for copy in [gain_copy] + row_copies + rest:
        copy.start()
    gain_copy.wait()
    for row in range(rows):
        row_copies[row].wait()
        values = fields_ref[row]
        mean = jnp.mean(values, axis=-1, keepdims=True)
        centred = values - mean
        var = jnp.mean(centred * centred, axis=-1, keepdims=True)
        out_ref[row * slots : (row + 1) * slots, :] = (
            centred * lax.rsqrt(var + EPS) * gain_ref[...]
        ).astype(jnp.bfloat16)
    for copy in rest:
        copy.wait()


def axial_project_kernel(own_ref, peer_ref, weights_ref, out_hbm, out_ref, sems):
    tokens = own_ref.shape[0]
    items, third, _ = out_ref.shape
    slots = third // 3
    rows = tokens // slots
    heads = AXIAL_HEADS // 2
    both = jnp.concatenate([own_ref[...], peer_ref[...]], axis=0)
    low = low_half((tokens, PAIR))
    copies = []
    for part in range(3):
        result = dot(both, weights_ref[part])
        if part == 0:
            result = result.astype(jnp.bfloat16).astype(jnp.float32) * SCALE
        for pair in range(heads // 2):
            span = slice(pair * PAIR, (pair + 1) * PAIR)
            own, peer = result[:tokens, span], result[tokens:, span]
            sides = (
                jnp.where(low, own, half_roll(peer)),
                jnp.where(low, half_roll(own), peer),
            )
            for side in range(2):
                packed = sides[side].astype(jnp.bfloat16)
                for row in range(rows):
                    out_ref[row * heads + pair * 2 + side, part * slots : (part + 1) * slots, :] = (
                        packed[row * slots : (row + 1) * slots]
                    )
        block = pl.ds(part * slots, slots)
        copies.append(
            pltpu.make_async_copy(out_ref.at[:, block], out_hbm.at[:, block], sems.at[part])
        )
        copies[part].start()
    for copy in copies:
        copy.wait()


def packed_part(ref, index):
    chips, third, _ = ref.shape
    slots = third // 3
    return ref[:, index * slots : (index + 1) * slots, :].reshape(chips * slots, PAIR)


def attend(for_own, for_peer, key_own, key_peer, values, out_ref):
    scores = jnp.concatenate([dot_t(for_own, key_own), dot_t(for_peer, key_peer)], axis=1)
    weights = jnp.exp(scores - jnp.max(scores, axis=-1, keepdims=True))
    total = jnp.sum(weights, axis=-1, keepdims=True)
    mixed = dot(weights.astype(jnp.bfloat16), values) / total
    out_ref[...] = mixed.astype(jnp.bfloat16).reshape(out_ref.shape)


def lane_masks(tokens):
    lane = lax.broadcasted_iota(jnp.int32, (tokens, PAIR), 1)
    bf16 = jnp.bfloat16
    return lane < HEAD_DIM, (lane == 0).astype(bf16), (lane == HEAD_DIM).astype(bf16)


def axial_peer_kernel(
    in_ref, bias_own_ref, bias_peer_ref, out_ref, key_own_ref, key_peer_ref, values_ref, rolled_ref
):
    tokens = bias_own_ref.shape[0]
    low, low_one, high_one = lane_masks(tokens)
    query, key, value = (packed_part(in_ref, index) for index in range(3))
    key_own_ref[...] = jnp.where(low, key, bias_own_ref[...])
    key_peer_ref[...] = jnp.where(low, bias_peer_ref[...], key)
    query_rolled, value_rolled = half_roll(query), half_roll(value)
    values_ref[:tokens] = value
    values_ref[tokens:] = value_rolled
    rolled_ref[...] = query_rolled
    attend(
        jnp.where(low, query_rolled, high_one),
        jnp.where(low, low_one, query),
        key_own_ref[...],
        key_peer_ref[...],
        jnp.concatenate([value_rolled, value], axis=0),
        out_ref,
    )


def axial_own_kernel(in_ref, key_own_ref, key_peer_ref, values_ref, rolled_ref, out_ref):
    low, low_one, high_one = lane_masks(rolled_ref.shape[0])
    attend(
        jnp.where(low, packed_part(in_ref, 0), high_one),
        jnp.where(low, low_one, rolled_ref[...]),
        key_own_ref[...],
        key_peer_ref[...],
        values_ref[...],
        out_ref,
    )


def join_kernel(low_ref, high_ref, out_ref):
    items, slots, _ = out_ref.shape
    low = low_half((items * slots, PAIR))
    joined = jnp.where(
        low, low_ref[...].reshape(items * slots, PAIR), high_ref[...].reshape(items * slots, PAIR)
    )
    out_ref[...] = joined.reshape(out_ref.shape)


def band_kernel(
    lat_count, lon_count, points_ref, mask_ref, own_ref, m2_ref, m1_ref, p1_ref, p2_ref,
    wq_hbm, wk_hbm, wv_hbm, out_ref, weights_ref, sems,
):
    first = AXIAL_HEADS * HEAD_DIM
    columns = pl.ds(first, weights_ref.shape[2])
    copies = [
        pltpu.make_async_copy(hbm.at[:, columns], weights_ref.at[place], sems.at[place])
        for place, hbm in enumerate((wk_hbm, wv_hbm, wq_hbm))
    ]
    for copy in copies:
        copy.start()
    lat = lax.axis_index("lat")
    lon = lax.axis_index("lon")
    tokens = own_ref.shape[0]
    slots = 32
    rows = tokens // slots
    bf16 = jnp.bfloat16
    own = own_ref[...]
    everything = jnp.concatenate([own, m2_ref[...], m1_ref[...], p1_ref[...], p2_ref[...]], axis=0)
    keys = everything.shape[0]
    slot = lax.broadcasted_iota(jnp.int32, (slots, PAIR), 0)
    blocks = []
    for offset in (0,) + OFFSETS:
        source = lat + offset
        held = jnp.clip(source, 0, lat_count - 1)
        if offset == 0:
            allowed = jnp.int32(1)
        else:
            column = offset + REACH if offset < 0 else offset + REACH - 1
            inside = (source >= 0) & (source < lat_count)
            allowed = jnp.where(inside & (mask_ref[column, lat] == 1), 1, 0)
        for row in range(rows):
            count = live_count(points_ref[held * rows + row], lon, lon_count) * allowed
            blocks.append(jnp.where(slot < count, 0.0, DEAD))
    bias = jnp.concatenate(blocks, axis=0)
    lane_k = lax.broadcasted_iota(jnp.int32, (keys, PAIR), 1)
    lane_q = lax.broadcasted_iota(jnp.int32, (tokens, PAIR), 1)
    low_k, low_q = lane_k < HEAD_DIM, lane_q < HEAD_DIM
    bias_high = jnp.where(lane_k == HEAD_DIM, bias, 0.0).astype(bf16)
    bias_low = jnp.where(lane_k == 0, bias, 0.0).astype(bf16)
    one_high = (lane_q == HEAD_DIM).astype(bf16)
    one_low = (lane_q == 0).astype(bf16)
    copies[0].wait()
    key = dot(everything, weights_ref[0]).astype(bf16)
    copies[1].wait()
    value = dot(everything, weights_ref[1]).astype(bf16)
    copies[2].wait()
    query = dot(own, weights_ref[2]).astype(bf16) * bf16(SCALE)
    for pair in range((HEADS - AXIAL_HEADS) // 2):
        span = slice(pair * PAIR, (pair + 1) * PAIR)
        q, k, v = query[:, span], key[:, span], value[:, span]
        scores = jnp.concatenate(
            [
                dot_t(jnp.where(low_q, q, one_high), jnp.where(low_k, k, bias_high)),
                dot_t(jnp.where(low_q, one_low, q), jnp.where(low_k, bias_low, k)),
            ],
            axis=0,
        )
        weights = jnp.exp(scores - jnp.max(scores, axis=-1, keepdims=True))
        total = jnp.sum(weights, axis=-1, keepdims=True)
        mixed = dot(weights.astype(bf16), v) / total
        out_ref[:, span] = jnp.where(low_q, mixed[:tokens], mixed[tokens:]).astype(bf16)


def band_out_kernel(
    lon_count, points_ref, fields_hbm, band_ref, w_hbm, out_ref, axial_w_ref, bias_own_ref, bias_peer_ref,
    fields_ref, w_ref, sems,
):
    lon = lax.axis_index("lon")
    core = lax.rem(lon, 2)
    chip = lon // 2
    rows, slots, width = fields_ref.shape
    depth = w_ref.shape[0]
    heads = AXIAL_HEADS // 2
    first = [
        pltpu.make_async_copy(w_hbm.at[pl.ds(depth, depth)], w_ref, sems.at[0]),
        pltpu.make_async_copy(fields_hbm, fields_ref, sems.at[1]),
    ]
    rest = []
    for head in range(heads):
        for side in range(2):
            source = (jnp.where(side == 0, core, 1 - core) * heads + head) * HEAD_DIM
            rest.append(
                pltpu.make_async_copy(
                    w_hbm.at[pl.ds(pl.multiple_of(source, HEAD_DIM), HEAD_DIM)],
                    axial_w_ref.at[pl.ds(head * PAIR + side * HEAD_DIM, HEAD_DIM)],
                    sems.at[2 + head * 2 + side],
                )
            )
    for copy in first + rest:
        copy.start()
    order = chip_order(lon_count // 2)
    points = points_ref[lax.axis_index("lat") * rows + place_of(chip, len(order)) // heads]
    slot = lax.broadcasted_iota(jnp.int32, (slots, PAIR), 0)
    lane = lax.broadcasted_iota(jnp.int32, (slots, PAIR), 1)
    for place, source in enumerate(order):
        part = pl.ds(place * slots, slots)
        dead_own = slot >= live_count(points, 2 * source + core, lon_count)
        dead_peer = slot >= live_count(points, 2 * source + 1 - core, lon_count)
        bias_own_ref[part, :] = jnp.where(dead_own & (lane == HEAD_DIM), DEAD, 0.0).astype(jnp.bfloat16)
        bias_peer_ref[part, :] = jnp.where(dead_peer & (lane == 0), DEAD, 0.0).astype(jnp.bfloat16)
    for copy in first:
        copy.wait()
    out_ref[...] = fields_ref[...].reshape(rows * slots, width) + dot(band_ref[...], w_ref[...])
    for copy in rest:
        copy.wait()


def finish_kernel(lon_count, points_ref, sum_ref, mixed_ref, w_ref, out_hbm, out_ref, sems):
    lon = lax.axis_index("lon")
    lat = lax.axis_index("lat")
    rows, slots, width = out_ref.shape
    heads = AXIAL_HEADS // 2
    mixed = jnp.concatenate(
        [
            jnp.concatenate([mixed_ref[row * heads + head] for head in range(heads)], axis=1)
            for row in range(rows)
        ],
        axis=0,
    )
    step = 256
    slot = lax.broadcasted_iota(jnp.int32, (slots, step), 0)
    counts = [live_count(points_ref[lat * rows + row], lon, lon_count) for row in range(rows)]
    copies = []
    for place in range(width // step):
        span = pl.ds(place * step, step)
        result = sum_ref[:, span] + dot(mixed, w_ref[:, span])
        for row in range(rows):
            out_ref[row, :, span] = jnp.where(
                slot < counts[row], result[row * slots : (row + 1) * slots], 0.0
            )
        copies.append(
            pltpu.make_async_copy(out_ref.at[:, :, span], out_hbm.at[:, :, span], sems.at[place])
        )
        copies[place].start()
    for copy in copies:
        copy.wait()


def call(kernel, shapes, specs, scratch=(), flops=0, out=VMEM):
    return pl.pallas_call(
        kernel,
        out_shape=[jax.ShapeDtypeStruct(shape, dtype) for shape, dtype in shapes],
        in_specs=specs,
        out_specs=[out] * len(shapes),
        scratch_shapes=scratch,
        compiler_params=pltpu.CompilerParams(vmem_limit_bytes=24 * 1024 * 1024),
        cost_estimate=pl.CostEstimate(flops=flops, transcendentals=0, bytes_accessed=0) if flops else None,
    )


def on_device(fields, row_points, band_mask, norm_gain, w_query, w_key, w_value, w_out):
    rows, slots, width = fields.shape
    lat_count = lax.axis_size("lat")
    lon_count = lax.axis_size("lon")
    tokens = rows * slots
    chips = lon_count // 2
    axial_width = AXIAL_HEADS * HEAD_DIM
    band_width = (HEADS - AXIAL_HEADS) * HEAD_DIM
    bf16, f32 = jnp.bfloat16, jnp.float32
    groups = [[2 * chip + core for chip in chip_order(chips)] for core in range(2)]
    swap = [(place, place + 1 - 2 * (place % 2)) for place in range(lon_count)]

    def in_hbm(*arrays):
        return [pltpu.with_memory_space_constraint(array, pltpu.HBM) for array in arrays]

    normed, weights = call(
        norm_kernel,
        [((tokens, width), bf16), ((3, width, axial_width // 2), bf16)],
        [HBM] * 5,
        [
            pltpu.VMEM((rows, slots, width), f32),
            pltpu.VMEM((1, width), f32),
            pltpu.SemaphoreType.DMA((4 + rows,)),
        ],
    )(*in_hbm(fields, norm_gain.reshape(1, width), w_query, w_key, w_value))
    peer = lax.ppermute(normed, "lon", swap)
    near = [
        lax.ppermute(
            normed, "lat", [(place, (place - offset) % lat_count) for place in range(lat_count)]
        )
        for offset in OFFSETS
    ]
    (packed,) = call(
        axial_project_kernel,
        [((chips, 3 * slots, PAIR), bf16)],
        [VMEM] * 3,
        [pltpu.VMEM((chips, 3 * slots, PAIR), bf16), pltpu.SemaphoreType.DMA((3,))],
        out=ANY,
    )(normed, peer, weights)
    row_head = lax.all_to_all(packed, "lon", 0, 0, axis_index_groups=groups, tiled=True)
    (band,) = call(
        functools.partial(band_kernel, lat_count, lon_count),
        [((tokens, band_width), bf16)],
        [SMEM, SMEM] + [VMEM] * 5 + [HBM] * 3,
        [
            pltpu.VMEM((3, width, band_width), bf16),
            pltpu.SemaphoreType.DMA((3,)),
        ],
        BAND_FLOPS,
    )(row_points, band_mask.T, normed, *near, *in_hbm(w_query, w_key, w_value))
    wide = ((chips * slots, PAIR), bf16)
    summed, axial_w, bias_own, bias_peer = call(
        functools.partial(band_out_kernel, lon_count),
        [((tokens, width), f32), ((axial_width, width), bf16), wide, wide],
        [SMEM, HBM, VMEM, HBM],
        [
            pltpu.VMEM((rows, slots, width), f32),
            pltpu.VMEM((band_width, width), bf16),
            pltpu.SemaphoreType.DMA((2 + AXIAL_HEADS,)),
        ],
        BAND_OUT_FLOPS,
    )(row_points, *in_hbm(fields), band, *in_hbm(w_out))
    item = ((chips, slots, PAIR), bf16)
    away, key_own, key_peer, values, rolled = call(
        axial_peer_kernel,
        [item, wide, wide, ((2 * chips * slots, PAIR), bf16), wide],
        [VMEM] * 3,
    )(row_head, bias_own, bias_peer)
    arrived = lax.ppermute(away, "lon", swap)
    (home,) = call(axial_own_kernel, [item], [VMEM] * 5, flops=AXIAL_FLOPS)(
        row_head, key_own, key_peer, values, rolled
    )
    (joined,) = call(join_kernel, [item], [VMEM] * 2)(home, arrived)
    mixed = lax.all_to_all(joined, "lon", 0, 0, axis_index_groups=groups, tiled=True)
    (out,) = call(
        functools.partial(finish_kernel, lon_count),
        [((rows, slots, width), f32)],
        [SMEM] + [VMEM] * 3,
        [pltpu.VMEM((rows, slots, width), f32), pltpu.SemaphoreType.DMA((4,))],
        out=ANY,
    )(row_points, summed, mixed, axial_w)
    return out


def solution(mesh):
    in_specs = (P("lat", "lon", None), P(), P(), P(), P(), P(), P(), P())
    out_specs = P("lat", "lon", None)
    return jax.shard_map(
        on_device, mesh=mesh, in_specs=in_specs, out_specs=out_specs, check_vma=False
    )
```

```python
import functools

import jax
import jax.numpy as jnp
from jax import lax
from jax.experimental import pallas as pl
from jax.experimental.pallas import tpu as pltpu
from jax.sharding import PartitionSpec as P

HEADS = 16
HEAD_DIM = 64
AXIAL_HEADS = 8
REACH = 2
EPS = 1e-05
DEAD = -1e30
PAIR = 2 * HEAD_DIM
SCALE = HEAD_DIM**-0.5
OFFSETS = (-2, -1, 1, 2)
AXIAL_FLOPS = 20_000_000_000
BAND_FLOPS = 20_000_000_000

VMEM = pl.BlockSpec(memory_space=pltpu.VMEM)
SMEM = pl.BlockSpec(memory_space=pltpu.SMEM)
HBM = pl.BlockSpec(memory_space=pltpu.HBM)
ANY = pl.BlockSpec(memory_space=pl.ANY)


def dot(a, b):
    return jnp.dot(a, b, preferred_element_type=jnp.float32)


def dot_t(a, b):
    return lax.dot_general(a, b, (((1,), (1,)), ((), ())), preferred_element_type=jnp.float32)


def half_roll(value):
    return pltpu.roll(value, HEAD_DIM, 1)


def low_half(shape):
    return lax.broadcasted_iota(jnp.int32, shape, 1) < HEAD_DIM


def chip_order(chips):
    half = chips // 2
    return [side * half + (z + half // 2) % half for side in range(2) for z in range(half)]


def place_of(chip, chips):
    half = chips // 2
    return chip // half * half + lax.rem(lax.rem(chip, half) + half // 2, half)


def live_count(points, tile, tiles):
    return points // tiles + (tile < points % tiles).astype(jnp.int32)


def norm_kernel(
    fields_hbm, gain_hbm, wq_hbm, wk_hbm, wv_hbm, out_ref, weights_ref, fields_ref, gain_ref, sems
):
    core = lax.rem(lax.axis_index("lon"), 2)
    width = weights_ref.shape[2]
    columns = pl.ds(pl.multiple_of(core * width, width), width)
    rows = fields_hbm.shape[0]
    slots = fields_hbm.shape[1]
    gain_copy = pltpu.make_async_copy(gain_hbm, gain_ref, sems.at[0])
    row_copies = [
        pltpu.make_async_copy(fields_hbm.at[row], fields_ref.at[row], sems.at[1 + row])
        for row in range(rows)
    ]
    rest = [
        pltpu.make_async_copy(hbm.at[:, columns], weights_ref.at[place], sems.at[1 + rows + place])
        for place, hbm in enumerate((wq_hbm, wk_hbm, wv_hbm))
    ]
    for copy in [gain_copy] + row_copies + rest:
        copy.start()
    gain_copy.wait()
    for row in range(rows):
        row_copies[row].wait()
        values = fields_ref[row]
        mean = jnp.mean(values, axis=-1, keepdims=True)
        centred = values - mean
        var = jnp.mean(centred * centred, axis=-1, keepdims=True)
        out_ref[row * slots : (row + 1) * slots, :] = (
            centred * lax.rsqrt(var + EPS) * gain_ref[...]
        ).astype(jnp.bfloat16)
    for copy in rest:
        copy.wait()


def axial_project_kernel(own_ref, peer_ref, weights_ref, out_hbm, out_ref, sems):
    tokens = own_ref.shape[0]
    items, third, _ = out_ref.shape
    slots = third // 3
    rows = tokens // slots
    heads = AXIAL_HEADS // 2
    both = jnp.concatenate([own_ref[...], peer_ref[...]], axis=0)
    low = low_half((tokens, PAIR))
    copies = []
    for part in range(3):
        result = dot(both, weights_ref[part])
        if part == 0:
            result = result.astype(jnp.bfloat16).astype(jnp.float32) * SCALE
        for pair in range(heads // 2):
            span = slice(pair * PAIR, (pair + 1) * PAIR)
            own, peer = result[:tokens, span], result[tokens:, span]
            sides = (
                jnp.where(low, own, half_roll(peer)),
                jnp.where(low, half_roll(own), peer),
            )
            for side in range(2):
                packed = sides[side].astype(jnp.bfloat16)
                for row in range(rows):
                    out_ref[row * heads + pair * 2 + side, part * slots : (part + 1) * slots, :] = (
                        packed[row * slots : (row + 1) * slots]
                    )
        block = pl.ds(part * slots, slots)
        copies.append(
            pltpu.make_async_copy(out_ref.at[:, block], out_hbm.at[:, block], sems.at[part])
        )
        copies[part].start()
    for copy in copies:
        copy.wait()


def packed_part(ref, index):
    chips, third, _ = ref.shape
    slots = third // 3
    return ref[:, index * slots : (index + 1) * slots, :].reshape(chips * slots, PAIR)


def attend(for_own, for_peer, key_own, key_peer, values, out_ref):
    scores = jnp.concatenate([dot_t(for_own, key_own), dot_t(for_peer, key_peer)], axis=1)
    weights = jnp.exp(scores - jnp.max(scores, axis=-1, keepdims=True))
    total = jnp.sum(weights, axis=-1, keepdims=True)
    mixed = dot(weights.astype(jnp.bfloat16), values) / total
    out_ref[...] = mixed.astype(jnp.bfloat16).reshape(out_ref.shape)


def lane_masks(tokens):
    lane = lax.broadcasted_iota(jnp.int32, (tokens, PAIR), 1)
    bf16 = jnp.bfloat16
    return lane < HEAD_DIM, (lane == 0).astype(bf16), (lane == HEAD_DIM).astype(bf16)


def axial_peer_kernel(
    in_ref, bias_own_ref, bias_peer_ref, out_ref, key_own_ref, key_peer_ref, values_ref, rolled_ref
):
    tokens = bias_own_ref.shape[0]
    low, low_one, high_one = lane_masks(tokens)
    query, key, value = (packed_part(in_ref, index) for index in range(3))
    key_own_ref[...] = jnp.where(low, key, bias_own_ref[...])
    key_peer_ref[...] = jnp.where(low, bias_peer_ref[...], key)
    query_rolled, value_rolled = half_roll(query), half_roll(value)
    values_ref[:tokens] = value
    values_ref[tokens:] = value_rolled
    rolled_ref[...] = query_rolled
    attend(
        jnp.where(low, query_rolled, high_one),
        jnp.where(low, low_one, query),
        key_own_ref[...],
        key_peer_ref[...],
        jnp.concatenate([value_rolled, value], axis=0),
        out_ref,
    )


def axial_own_kernel(in_ref, key_own_ref, key_peer_ref, values_ref, rolled_ref, out_ref):
    low, low_one, high_one = lane_masks(rolled_ref.shape[0])
    attend(
        jnp.where(low, packed_part(in_ref, 0), high_one),
        jnp.where(low, low_one, rolled_ref[...]),
        key_own_ref[...],
        key_peer_ref[...],
        values_ref[...],
        out_ref,
    )


def join_kernel(low_ref, high_ref, out_ref):
    items, slots, _ = out_ref.shape
    low = low_half((items * slots, PAIR))
    joined = jnp.where(
        low, low_ref[...].reshape(items * slots, PAIR), high_ref[...].reshape(items * slots, PAIR)
    )
    out_ref[...] = joined.reshape(out_ref.shape)


def band_kernel(
    lat_count, lon_count, points_ref, mask_ref, own_ref, m2_ref, m1_ref, p1_ref, p2_ref,
    wq_hbm, wk_hbm, wv_hbm, fields_hbm, w_hbm,
    out_ref, axial_w_ref, bias_own_ref, bias_peer_ref,
    weights_ref, fields_ref, w_ref, band_ref, sems,
):
    first = AXIAL_HEADS * HEAD_DIM
    columns = pl.ds(first, weights_ref.shape[2])
    copies = [
        pltpu.make_async_copy(hbm.at[:, columns], weights_ref.at[place], sems.at[place])
        for place, hbm in enumerate((wk_hbm, wv_hbm, wq_hbm))
    ]
    late = [
        pltpu.make_async_copy(w_hbm.at[pl.ds(first, w_ref.shape[0])], w_ref, sems.at[3]),
        pltpu.make_async_copy(fields_hbm, fields_ref, sems.at[4]),
    ]
    lat = lax.axis_index("lat")
    lon = lax.axis_index("lon")
    core = lax.rem(lon, 2)
    heads = AXIAL_HEADS // 2
    for head in range(heads):
        for side in range(2):
            source = (jnp.where(side == 0, core, 1 - core) * heads + head) * HEAD_DIM
            late.append(
                pltpu.make_async_copy(
                    w_hbm.at[pl.ds(pl.multiple_of(source, HEAD_DIM), HEAD_DIM)],
                    axial_w_ref.at[pl.ds(head * PAIR + side * HEAD_DIM, HEAD_DIM)],
                    sems.at[5 + head * 2 + side],
                )
            )
    for copy in copies + late:
        copy.start()
    tokens = own_ref.shape[0]
    slots = 32
    rows = tokens // slots
    bf16 = jnp.bfloat16
    own = own_ref[...]
    everything = jnp.concatenate([own, m2_ref[...], m1_ref[...], p1_ref[...], p2_ref[...]], axis=0)
    keys = everything.shape[0]
    slot = lax.broadcasted_iota(jnp.int32, (slots, PAIR), 0)
    blocks = []
    for offset in (0,) + OFFSETS:
        source = lat + offset
        held = jnp.clip(source, 0, lat_count - 1)
        if offset == 0:
            allowed = jnp.int32(1)
        else:
            column = offset + REACH if offset < 0 else offset + REACH - 1
            inside = (source >= 0) & (source < lat_count)
            allowed = jnp.where(inside & (mask_ref[column, lat] == 1), 1, 0)
        for row in range(rows):
            count = live_count(points_ref[held * rows + row], lon, lon_count) * allowed
            blocks.append(jnp.where(slot < count, 0.0, DEAD))
    bias = jnp.concatenate(blocks, axis=0)
    lane_k = lax.broadcasted_iota(jnp.int32, (keys, PAIR), 1)
    lane_q = lax.broadcasted_iota(jnp.int32, (tokens, PAIR), 1)
    low_k, low_q = lane_k < HEAD_DIM, lane_q < HEAD_DIM
    bias_high = jnp.where(lane_k == HEAD_DIM, bias, 0.0).astype(bf16)
    bias_low = jnp.where(lane_k == 0, bias, 0.0).astype(bf16)
    one_high = (lane_q == HEAD_DIM).astype(bf16)
    one_low = (lane_q == 0).astype(bf16)
    copies[0].wait()
    key = dot(everything, weights_ref[0]).astype(bf16)
    copies[1].wait()
    value = dot(everything, weights_ref[1]).astype(bf16)
    copies[2].wait()
    query = dot(own, weights_ref[2]).astype(bf16) * bf16(SCALE)
    for pair in range((HEADS - AXIAL_HEADS) // 2):
        span = slice(pair * PAIR, (pair + 1) * PAIR)
        q, k, v = query[:, span], key[:, span], value[:, span]
        scores = jnp.concatenate(
            [
                dot_t(jnp.where(low_q, q, one_high), jnp.where(low_k, k, bias_high)),
                dot_t(jnp.where(low_q, one_low, q), jnp.where(low_k, bias_low, k)),
            ],
            axis=0,
        )
        weights = jnp.exp(scores - jnp.max(scores, axis=-1, keepdims=True))
        total = jnp.sum(weights, axis=-1, keepdims=True)
        mixed = dot(weights.astype(bf16), v) / total
        band_ref[:, span] = jnp.where(low_q, mixed[:tokens], mixed[tokens:]).astype(bf16)
    order = chip_order(lon_count // 2)
    points = points_ref[lat * rows + place_of(lon // 2, len(order)) // heads]
    lane = lax.broadcasted_iota(jnp.int32, (slots, PAIR), 1)
    for place, source in enumerate(order):
        part = pl.ds(place * slots, slots)
        dead_own = slot >= live_count(points, 2 * source + core, lon_count)
        dead_peer = slot >= live_count(points, 2 * source + 1 - core, lon_count)
        bias_own_ref[part, :] = jnp.where(dead_own & (lane == HEAD_DIM), DEAD, 0.0).astype(bf16)
        bias_peer_ref[part, :] = jnp.where(dead_peer & (lane == 0), DEAD, 0.0).astype(bf16)
    for copy in late[:2]:
        copy.wait()
    width = fields_ref.shape[2]
    out_ref[...] = fields_ref[...].reshape(tokens, width) + dot(band_ref[...], w_ref[...])
    for copy in late[2:]:
        copy.wait()


def finish_kernel(lon_count, points_ref, sum_ref, mixed_ref, w_ref, out_hbm, out_ref, sems):
    lon = lax.axis_index("lon")
    lat = lax.axis_index("lat")
    rows, slots, width = out_ref.shape
    heads = AXIAL_HEADS // 2
    mixed = jnp.concatenate(
        [
            jnp.concatenate([mixed_ref[row * heads + head] for head in range(heads)], axis=1)
            for row in range(rows)
        ],
        axis=0,
    )
    step = 256
    slot = lax.broadcasted_iota(jnp.int32, (slots, step), 0)
    counts = [live_count(points_ref[lat * rows + row], lon, lon_count) for row in range(rows)]
    copies = []
    for place in range(width // step):
        span = pl.ds(place * step, step)
        result = sum_ref[:, span] + dot(mixed, w_ref[:, span])
        for row in range(rows):
            out_ref[row, :, span] = jnp.where(
                slot < counts[row], result[row * slots : (row + 1) * slots], 0.0
            )
        copies.append(
            pltpu.make_async_copy(out_ref.at[:, :, span], out_hbm.at[:, :, span], sems.at[place])
        )
        copies[place].start()
    for copy in copies:
        copy.wait()


def call(kernel, shapes, specs, scratch=(), flops=0, out=VMEM):
    return pl.pallas_call(
        kernel,
        out_shape=[jax.ShapeDtypeStruct(shape, dtype) for shape, dtype in shapes],
        in_specs=specs,
        out_specs=[out] * len(shapes),
        scratch_shapes=scratch,
        compiler_params=pltpu.CompilerParams(vmem_limit_bytes=24 * 1024 * 1024),
        cost_estimate=pl.CostEstimate(flops=flops, transcendentals=0, bytes_accessed=0) if flops else None,
    )


def on_device(fields, row_points, band_mask, norm_gain, w_query, w_key, w_value, w_out):
    rows, slots, width = fields.shape
    lat_count = lax.axis_size("lat")
    lon_count = lax.axis_size("lon")
    tokens = rows * slots
    chips = lon_count // 2
    axial_width = AXIAL_HEADS * HEAD_DIM
    band_width = (HEADS - AXIAL_HEADS) * HEAD_DIM
    bf16, f32 = jnp.bfloat16, jnp.float32
    groups = [[2 * chip + core for chip in chip_order(chips)] for core in range(2)]
    swap = [(place, place + 1 - 2 * (place % 2)) for place in range(lon_count)]

    def in_hbm(*arrays):
        return [pltpu.with_memory_space_constraint(array, pltpu.HBM) for array in arrays]

    normed, weights = call(
        norm_kernel,
        [((tokens, width), bf16), ((3, width, axial_width // 2), bf16)],
        [HBM] * 5,
        [
            pltpu.VMEM((rows, slots, width), f32),
            pltpu.VMEM((1, width), f32),
            pltpu.SemaphoreType.DMA((4 + rows,)),
        ],
    )(*in_hbm(fields, norm_gain.reshape(1, width), w_query, w_key, w_value))
    peer = lax.ppermute(normed, "lon", swap)
    near = [
        lax.ppermute(
            normed, "lat", [(place, (place - offset) % lat_count) for place in range(lat_count)]
        )
        for offset in OFFSETS
    ]
    (packed,) = call(
        axial_project_kernel,
        [((chips, 3 * slots, PAIR), bf16)],
        [VMEM] * 3,
        [pltpu.VMEM((chips, 3 * slots, PAIR), bf16), pltpu.SemaphoreType.DMA((3,))],
        out=ANY,
    )(normed, peer, weights)
    row_head = lax.all_to_all(packed, "lon", 0, 0, axis_index_groups=groups, tiled=True)
    wide = ((chips * slots, PAIR), bf16)
    summed, axial_w, bias_own, bias_peer = call(
        functools.partial(band_kernel, lat_count, lon_count),
        [((tokens, width), f32), ((axial_width, width), bf16), wide, wide],
        [SMEM, SMEM] + [VMEM] * 5 + [HBM] * 5,
        [
            pltpu.VMEM((3, width, band_width), bf16),
            pltpu.VMEM((rows, slots, width), f32),
            pltpu.VMEM((band_width, width), bf16),
            pltpu.VMEM((tokens, band_width), bf16),
            pltpu.SemaphoreType.DMA((5 + AXIAL_HEADS,)),
        ],
        BAND_FLOPS,
    )(row_points, band_mask.T, normed, *near, *in_hbm(w_query, w_key, w_value, fields, w_out))
    item = ((chips, slots, PAIR), bf16)
    away, key_own, key_peer, values, rolled = call(
        axial_peer_kernel,
        [item, wide, wide, ((2 * chips * slots, PAIR), bf16), wide],
        [VMEM] * 3,
    )(row_head, bias_own, bias_peer)
    arrived = lax.ppermute(away, "lon", swap)
    (home,) = call(axial_own_kernel, [item], [VMEM] * 5, flops=AXIAL_FLOPS)(
        row_head, key_own, key_peer, values, rolled
    )
    (joined,) = call(join_kernel, [item], [VMEM] * 2)(home, arrived)
    mixed = lax.all_to_all(joined, "lon", 0, 0, axis_index_groups=groups, tiled=True)
    (out,) = call(
        functools.partial(finish_kernel, lon_count),
        [((rows, slots, width), f32)],
        [SMEM] + [VMEM] * 3,
        [pltpu.VMEM((rows, slots, width), f32), pltpu.SemaphoreType.DMA((4,))],
        out=ANY,
    )(row_points, summed, mixed, axial_w)
    return out


def solution(mesh):
    in_specs = (P("lat", "lon", None), P(), P(), P(), P(), P(), P(), P())
    out_specs = P("lat", "lon", None)
    return jax.shard_map(
        on_device, mesh=mesh, in_specs=in_specs, out_specs=out_specs, check_vma=False
    )
```

```python
import functools

import jax
import jax.numpy as jnp
from jax import lax
from jax.experimental import pallas as pl
from jax.experimental.pallas import tpu as pltpu
from jax.sharding import PartitionSpec as P

HEADS = 16
HEAD_DIM = 64
AXIAL_HEADS = 8
REACH = 2
EPS = 1e-05
DEAD = -1e30
PAIR = 2 * HEAD_DIM
SCALE = HEAD_DIM**-0.5
OFFSETS = (-2, -1, 1, 2)
AXIAL_FLOPS = 20_000_000_000
BAND_FLOPS = 20_000_000_000

VMEM = pl.BlockSpec(memory_space=pltpu.VMEM)
SMEM = pl.BlockSpec(memory_space=pltpu.SMEM)
HBM = pl.BlockSpec(memory_space=pltpu.HBM)
ANY = pl.BlockSpec(memory_space=pl.ANY)


def dot(a, b):
    return jnp.dot(a, b, preferred_element_type=jnp.float32)


def dot_t(a, b):
    return lax.dot_general(a, b, (((1,), (1,)), ((), ())), preferred_element_type=jnp.float32)


def half_roll(value):
    return pltpu.roll(value, HEAD_DIM, 1)


def low_half(shape):
    return lax.broadcasted_iota(jnp.int32, shape, 1) < HEAD_DIM


def chip_order(chips):
    half = chips // 2
    return [side * half + (z + half // 2) % half for side in (1, 0) for z in range(half)]


def place_of(chip, chips):
    half = chips // 2
    return (1 - chip // half) * half + lax.rem(lax.rem(chip, half) + half // 2, half)


def live_count(points, tile, tiles):
    return points // tiles + (tile < points % tiles).astype(jnp.int32)


def norm_kernel(
    fields_hbm, gain_hbm, wq_hbm, wk_hbm, wv_hbm, out_ref, weights_ref, fields_ref, gain_ref, sems
):
    core = lax.rem(lax.axis_index("lon"), 2)
    width = weights_ref.shape[2]
    columns = pl.ds(pl.multiple_of(core * width, width), width)
    rows = fields_hbm.shape[0]
    slots = fields_hbm.shape[1]
    gain_copy = pltpu.make_async_copy(gain_hbm, gain_ref, sems.at[0])
    row_copies = [
        pltpu.make_async_copy(fields_hbm.at[row], fields_ref.at[row], sems.at[1 + row])
        for row in range(rows)
    ]
    rest = [
        pltpu.make_async_copy(hbm.at[:, columns], weights_ref.at[place], sems.at[1 + rows + place])
        for place, hbm in enumerate((wq_hbm, wk_hbm, wv_hbm))
    ]
    for copy in [gain_copy] + row_copies + rest:
        copy.start()
    gain_copy.wait()
    for row in range(rows):
        row_copies[row].wait()
        values = fields_ref[row]
        mean = jnp.mean(values, axis=-1, keepdims=True)
        centred = values - mean
        var = jnp.mean(centred * centred, axis=-1, keepdims=True)
        out_ref[row * slots : (row + 1) * slots, :] = (
            centred * lax.rsqrt(var + EPS) * gain_ref[...]
        ).astype(jnp.bfloat16)
    for copy in rest:
        copy.wait()


def axial_project_kernel(own_ref, peer_ref, weights_ref, out_hbm, out_ref, sems):
    tokens = own_ref.shape[0]
    items, third, _ = out_ref.shape
    slots = third // 3
    rows = tokens // slots
    heads = AXIAL_HEADS // 2
    both = jnp.concatenate([own_ref[...], peer_ref[...]], axis=0)
    low = low_half((tokens, PAIR))
    copies = []
    for part in range(3):
        result = dot(both, weights_ref[part])
        if part == 0:
            result = result.astype(jnp.bfloat16).astype(jnp.float32) * SCALE
        for pair in range(heads // 2):
            span = slice(pair * PAIR, (pair + 1) * PAIR)
            own, peer = result[:tokens, span], result[tokens:, span]
            sides = (
                jnp.where(low, own, half_roll(peer)),
                jnp.where(low, half_roll(own), peer),
            )
            for side in range(2):
                packed = sides[side].astype(jnp.bfloat16)
                for row in range(rows):
                    out_ref[row * heads + pair * 2 + side, part * slots : (part + 1) * slots, :] = (
                        packed[row * slots : (row + 1) * slots]
                    )
        block = pl.ds(part * slots, slots)
        copies.append(
            pltpu.make_async_copy(out_ref.at[:, block], out_hbm.at[:, block], sems.at[part])
        )
        copies[part].start()
    for copy in copies:
        copy.wait()


def packed_part(ref, index):
    chips, third, _ = ref.shape
    slots = third // 3
    return ref[:, index * slots : (index + 1) * slots, :].reshape(chips * slots, PAIR)


def attend(for_own, for_peer, key_own, key_peer, values, out_ref):
    scores = jnp.concatenate([dot_t(for_own, key_own), dot_t(for_peer, key_peer)], axis=1)
    weights = jnp.exp(scores - jnp.max(scores, axis=-1, keepdims=True))
    total = jnp.sum(weights, axis=-1, keepdims=True)
    mixed = dot(weights.astype(jnp.bfloat16), values) / total
    out_ref[...] = mixed.astype(jnp.bfloat16).reshape(out_ref.shape)


def lane_masks(tokens):
    lane = lax.broadcasted_iota(jnp.int32, (tokens, PAIR), 1)
    bf16 = jnp.bfloat16
    return lane < HEAD_DIM, (lane == 0).astype(bf16), (lane == HEAD_DIM).astype(bf16)


def axial_peer_kernel(
    in_ref, bias_own_ref, bias_peer_ref, out_ref, key_own_ref, key_peer_ref, values_ref, rolled_ref
):
    tokens = bias_own_ref.shape[0]
    low, low_one, high_one = lane_masks(tokens)
    query, key, value = (packed_part(in_ref, index) for index in range(3))
    key_own_ref[...] = jnp.where(low, key, bias_own_ref[...])
    key_peer_ref[...] = jnp.where(low, bias_peer_ref[...], key)
    query_rolled, value_rolled = half_roll(query), half_roll(value)
    values_ref[:tokens] = value
    values_ref[tokens:] = value_rolled
    rolled_ref[...] = query_rolled
    attend(
        jnp.where(low, query_rolled, high_one),
        jnp.where(low, low_one, query),
        key_own_ref[...],
        key_peer_ref[...],
        jnp.concatenate([value_rolled, value], axis=0),
        out_ref,
    )


def axial_own_kernel(in_ref, key_own_ref, key_peer_ref, values_ref, rolled_ref, out_ref):
    low, low_one, high_one = lane_masks(rolled_ref.shape[0])
    attend(
        jnp.where(low, packed_part(in_ref, 0), high_one),
        jnp.where(low, low_one, rolled_ref[...]),
        key_own_ref[...],
        key_peer_ref[...],
        values_ref[...],
        out_ref,
    )


def join_kernel(low_ref, high_ref, out_ref):
    items, slots, _ = out_ref.shape
    low = low_half((items * slots, PAIR))
    joined = jnp.where(
        low, low_ref[...].reshape(items * slots, PAIR), high_ref[...].reshape(items * slots, PAIR)
    )
    out_ref[...] = joined.reshape(out_ref.shape)


def band_kernel(
    lat_count, lon_count, points_ref, mask_ref, own_ref, m2_ref, m1_ref, p1_ref, p2_ref,
    wq_hbm, wk_hbm, wv_hbm, fields_hbm, w_hbm,
    out_ref, axial_w_ref, bias_own_ref, bias_peer_ref,
    weights_ref, fields_ref, w_ref, band_ref, sems,
):
    first = AXIAL_HEADS * HEAD_DIM
    columns = pl.ds(first, weights_ref.shape[2])
    copies = [
        pltpu.make_async_copy(hbm.at[:, columns], weights_ref.at[place], sems.at[place])
        for place, hbm in enumerate((wk_hbm, wv_hbm, wq_hbm))
    ]
    late = [
        pltpu.make_async_copy(w_hbm.at[pl.ds(first, w_ref.shape[0])], w_ref, sems.at[3]),
        pltpu.make_async_copy(fields_hbm, fields_ref, sems.at[4]),
    ]
    lat = lax.axis_index("lat")
    lon = lax.axis_index("lon")
    core = lax.rem(lon, 2)
    heads = AXIAL_HEADS // 2
    for head in range(heads):
        for side in range(2):
            source = (jnp.where(side == 0, core, 1 - core) * heads + head) * HEAD_DIM
            late.append(
                pltpu.make_async_copy(
                    w_hbm.at[pl.ds(pl.multiple_of(source, HEAD_DIM), HEAD_DIM)],
                    axial_w_ref.at[pl.ds(head * PAIR + side * HEAD_DIM, HEAD_DIM)],
                    sems.at[5 + head * 2 + side],
                )
            )
    for copy in copies + late:
        copy.start()
    tokens = own_ref.shape[0]
    slots = 32
    rows = tokens // slots
    bf16 = jnp.bfloat16
    own = own_ref[...]
    everything = jnp.concatenate([own, m2_ref[...], m1_ref[...], p1_ref[...], p2_ref[...]], axis=0)
    keys = everything.shape[0]
    slot = lax.broadcasted_iota(jnp.int32, (slots, PAIR), 0)
    blocks = []
    for offset in (0,) + OFFSETS:
        source = lat + offset
        held = jnp.clip(source, 0, lat_count - 1)
        if offset == 0:
            allowed = jnp.int32(1)
        else:
            column = offset + REACH if offset < 0 else offset + REACH - 1
            inside = (source >= 0) & (source < lat_count)
            allowed = jnp.where(inside & (mask_ref[column, lat] == 1), 1, 0)
        for row in range(rows):
            count = live_count(points_ref[held * rows + row], lon, lon_count) * allowed
            blocks.append(jnp.where(slot < count, 0.0, DEAD))
    bias = jnp.concatenate(blocks, axis=0)
    lane_k = lax.broadcasted_iota(jnp.int32, (keys, PAIR), 1)
    lane_q = lax.broadcasted_iota(jnp.int32, (tokens, PAIR), 1)
    low_k, low_q = lane_k < HEAD_DIM, lane_q < HEAD_DIM
    bias_high = jnp.where(lane_k == HEAD_DIM, bias, 0.0).astype(bf16)
    bias_low = jnp.where(lane_k == 0, bias, 0.0).astype(bf16)
    one_high = (lane_q == HEAD_DIM).astype(bf16)
    one_low = (lane_q == 0).astype(bf16)
    copies[0].wait()
    key = dot(everything, weights_ref[0]).astype(bf16)
    copies[1].wait()
    value = dot(everything, weights_ref[1]).astype(bf16)
    copies[2].wait()
    query = dot(own, weights_ref[2]).astype(bf16) * bf16(SCALE)
    for pair in range((HEADS - AXIAL_HEADS) // 2):
        span = slice(pair * PAIR, (pair + 1) * PAIR)
        q, k, v = query[:, span], key[:, span], value[:, span]
        scores = jnp.concatenate(
            [
                dot_t(jnp.where(low_q, q, one_high), jnp.where(low_k, k, bias_high)),
                dot_t(jnp.where(low_q, one_low, q), jnp.where(low_k, bias_low, k)),
            ],
            axis=0,
        )
        weights = jnp.exp(scores - jnp.max(scores, axis=-1, keepdims=True))
        total = jnp.sum(weights, axis=-1, keepdims=True)
        mixed = dot(weights.astype(bf16), v) / total
        band_ref[:, span] = jnp.where(low_q, mixed[:tokens], mixed[tokens:]).astype(bf16)
    order = chip_order(lon_count // 2)
    points = points_ref[lat * rows + place_of(lon // 2, len(order)) // heads]
    lane = lax.broadcasted_iota(jnp.int32, (slots, PAIR), 1)
    for place, source in enumerate(order):
        part = pl.ds(place * slots, slots)
        dead_own = slot >= live_count(points, 2 * source + core, lon_count)
        dead_peer = slot >= live_count(points, 2 * source + 1 - core, lon_count)
        bias_own_ref[part, :] = jnp.where(dead_own & (lane == HEAD_DIM), DEAD, 0.0).astype(bf16)
        bias_peer_ref[part, :] = jnp.where(dead_peer & (lane == 0), DEAD, 0.0).astype(bf16)
    for copy in late[:2]:
        copy.wait()
    width = fields_ref.shape[2]
    out_ref[...] = fields_ref[...].reshape(tokens, width) + dot(band_ref[...], w_ref[...])
    for copy in late[2:]:
        copy.wait()


def finish_kernel(lon_count, points_ref, sum_ref, mixed_ref, w_ref, out_hbm, out_ref, sems):
    lon = lax.axis_index("lon")
    lat = lax.axis_index("lat")
    rows, slots, width = out_ref.shape
    heads = AXIAL_HEADS // 2
    mixed = jnp.concatenate(
        [
            jnp.concatenate([mixed_ref[row * heads + head] for head in range(heads)], axis=1)
            for row in range(rows)
        ],
        axis=0,
    )
    step = 256
    slot = lax.broadcasted_iota(jnp.int32, (slots, step), 0)
    counts = [live_count(points_ref[lat * rows + row], lon, lon_count) for row in range(rows)]
    copies = []
    for place in range(width // step):
        span = pl.ds(place * step, step)
        result = sum_ref[:, span] + dot(mixed, w_ref[:, span])
        for row in range(rows):
            out_ref[row, :, span] = jnp.where(
                slot < counts[row], result[row * slots : (row + 1) * slots], 0.0
            )
        copies.append(
            pltpu.make_async_copy(out_ref.at[:, :, span], out_hbm.at[:, :, span], sems.at[place])
        )
        copies[place].start()
    for copy in copies:
        copy.wait()


def call(kernel, shapes, specs, scratch=(), flops=0, out=VMEM):
    return pl.pallas_call(
        kernel,
        out_shape=[jax.ShapeDtypeStruct(shape, dtype) for shape, dtype in shapes],
        in_specs=specs,
        out_specs=[out] * len(shapes),
        scratch_shapes=scratch,
        compiler_params=pltpu.CompilerParams(vmem_limit_bytes=24 * 1024 * 1024),
        cost_estimate=pl.CostEstimate(flops=flops, transcendentals=0, bytes_accessed=0) if flops else None,
    )


def on_device(fields, row_points, band_mask, norm_gain, w_query, w_key, w_value, w_out):
    rows, slots, width = fields.shape
    lat_count = lax.axis_size("lat")
    lon_count = lax.axis_size("lon")
    tokens = rows * slots
    chips = lon_count // 2
    axial_width = AXIAL_HEADS * HEAD_DIM
    band_width = (HEADS - AXIAL_HEADS) * HEAD_DIM
    bf16, f32 = jnp.bfloat16, jnp.float32
    groups = [[2 * chip + core for chip in chip_order(chips)] for core in range(2)]
    swap = [(place, place + 1 - 2 * (place % 2)) for place in range(lon_count)]

    def in_hbm(*arrays):
        return [pltpu.with_memory_space_constraint(array, pltpu.HBM) for array in arrays]

    normed, weights = call(
        norm_kernel,
        [((tokens, width), bf16), ((3, width, axial_width // 2), bf16)],
        [HBM] * 5,
        [
            pltpu.VMEM((rows, slots, width), f32),
            pltpu.VMEM((1, width), f32),
            pltpu.SemaphoreType.DMA((4 + rows,)),
        ],
    )(*in_hbm(fields, norm_gain.reshape(1, width), w_query, w_key, w_value))
    peer = lax.ppermute(normed, "lon", swap)
    near = [
        lax.ppermute(
            normed, "lat", [(place, (place - offset) % lat_count) for place in range(lat_count)]
        )
        for offset in OFFSETS
    ]
    (packed,) = call(
        axial_project_kernel,
        [((chips, 3 * slots, PAIR), bf16)],
        [VMEM] * 3,
        [pltpu.VMEM((chips, 3 * slots, PAIR), bf16), pltpu.SemaphoreType.DMA((3,))],
        out=ANY,
    )(normed, peer, weights)
    row_head = lax.all_to_all(packed, "lon", 0, 0, axis_index_groups=groups, tiled=True)
    wide = ((chips * slots, PAIR), bf16)
    summed, axial_w, bias_own, bias_peer = call(
        functools.partial(band_kernel, lat_count, lon_count),
        [((tokens, width), f32), ((axial_width, width), bf16), wide, wide],
        [SMEM, SMEM] + [VMEM] * 5 + [HBM] * 5,
        [
            pltpu.VMEM((3, width, band_width), bf16),
            pltpu.VMEM((rows, slots, width), f32),
            pltpu.VMEM((band_width, width), bf16),
            pltpu.VMEM((tokens, band_width), bf16),
            pltpu.SemaphoreType.DMA((5 + AXIAL_HEADS,)),
        ],
        BAND_FLOPS,
    )(row_points, band_mask.T, normed, *near, *in_hbm(w_query, w_key, w_value, fields, w_out))
    item = ((chips, slots, PAIR), bf16)
    away, key_own, key_peer, values, rolled = call(
        axial_peer_kernel,
        [item, wide, wide, ((2 * chips * slots, PAIR), bf16), wide],
        [VMEM] * 3,
    )(row_head, bias_own, bias_peer)
    arrived = lax.ppermute(away, "lon", swap)
    (home,) = call(axial_own_kernel, [item], [VMEM] * 5, flops=AXIAL_FLOPS)(
        row_head, key_own, key_peer, values, rolled
    )
    (joined,) = call(join_kernel, [item], [VMEM] * 2)(home, arrived)
    mixed = lax.all_to_all(joined, "lon", 0, 0, axis_index_groups=groups, tiled=True)
    (out,) = call(
        functools.partial(finish_kernel, lon_count),
        [((rows, slots, width), f32)],
        [SMEM] + [VMEM] * 3,
        [pltpu.VMEM((rows, slots, width), f32), pltpu.SemaphoreType.DMA((4,))],
        out=ANY,
    )(row_points, summed, mixed, axial_w)
    return out


def solution(mesh):
    in_specs = (P("lat", "lon", None), P(), P(), P(), P(), P(), P(), P())
    out_specs = P("lat", "lon", None)
    return jax.shard_map(
        on_device, mesh=mesh, in_specs=in_specs, out_specs=out_specs, check_vma=False
    )
```

```python
import functools

import jax
import jax.numpy as jnp
from jax import lax
from jax.experimental import pallas as pl
from jax.experimental.pallas import tpu as pltpu
from jax.sharding import PartitionSpec as P

HEADS = 16
HEAD_DIM = 64
AXIAL_HEADS = 8
REACH = 2
EPS = 1e-05
DEAD = -1e30
PAIR = 2 * HEAD_DIM
SCALE = HEAD_DIM**-0.5
OFFSETS = (-1, 1, -2, 2)
AXIAL_FLOPS = 20_000_000_000
BAND_FLOPS = 20_000_000_000

VMEM = pl.BlockSpec(memory_space=pltpu.VMEM)
SMEM = pl.BlockSpec(memory_space=pltpu.SMEM)
HBM = pl.BlockSpec(memory_space=pltpu.HBM)
ANY = pl.BlockSpec(memory_space=pl.ANY)


def dot(a, b):
    return jnp.dot(a, b, preferred_element_type=jnp.float32)


def dot_t(a, b):
    return lax.dot_general(a, b, (((1,), (1,)), ((), ())), preferred_element_type=jnp.float32)


def half_roll(value):
    return pltpu.roll(value, HEAD_DIM, 1)


def low_half(shape):
    return lax.broadcasted_iota(jnp.int32, shape, 1) < HEAD_DIM


def chip_order(chips):
    half = chips // 2
    return [side * half + (z + half // 2) % half for side in (1, 0) for z in range(half)]


def place_of(chip, chips):
    half = chips // 2
    return (1 - chip // half) * half + lax.rem(lax.rem(chip, half) + half // 2, half)


def live_count(points, tile, tiles):
    return points // tiles + (tile < points % tiles).astype(jnp.int32)


def norm_kernel(
    fields_hbm, gain_hbm, wq_hbm, wk_hbm, wv_hbm, out_ref, weights_ref, fields_ref, gain_ref, sems
):
    core = lax.rem(lax.axis_index("lon"), 2)
    width = weights_ref.shape[2]
    columns = pl.ds(pl.multiple_of(core * width, width), width)
    rows = fields_hbm.shape[0]
    slots = fields_hbm.shape[1]
    gain_copy = pltpu.make_async_copy(gain_hbm, gain_ref, sems.at[0])
    row_copies = [
        pltpu.make_async_copy(fields_hbm.at[row], fields_ref.at[row], sems.at[1 + row])
        for row in range(rows)
    ]
    rest = [
        pltpu.make_async_copy(hbm.at[:, columns], weights_ref.at[place], sems.at[1 + rows + place])
        for place, hbm in enumerate((wq_hbm, wk_hbm, wv_hbm))
    ]
    for copy in [gain_copy] + row_copies + rest:
        copy.start()
    gain_copy.wait()
    for row in range(rows):
        row_copies[row].wait()
        values = fields_ref[row]
        mean = jnp.mean(values, axis=-1, keepdims=True)
        centred = values - mean
        var = jnp.mean(centred * centred, axis=-1, keepdims=True)
        out_ref[row * slots : (row + 1) * slots, :] = (
            centred * lax.rsqrt(var + EPS) * gain_ref[...]
        ).astype(jnp.bfloat16)
    for copy in rest:
        copy.wait()


def axial_project_kernel(own_ref, peer_ref, weights_ref, out_hbm, out_ref, sems):
    tokens = own_ref.shape[0]
    items, third, _ = out_ref.shape
    slots = third // 3
    rows = tokens // slots
    heads = AXIAL_HEADS // 2
    both = jnp.concatenate([own_ref[...], peer_ref[...]], axis=0)
    low = low_half((tokens, PAIR))
    copies = []
    for part in range(3):
        result = dot(both, weights_ref[part])
        if part == 0:
            result = result.astype(jnp.bfloat16).astype(jnp.float32) * SCALE
        for pair in range(heads // 2):
            span = slice(pair * PAIR, (pair + 1) * PAIR)
            own, peer = result[:tokens, span], result[tokens:, span]
            sides = (
                jnp.where(low, own, half_roll(peer)),
                jnp.where(low, half_roll(own), peer),
            )
            for side in range(2):
                packed = sides[side].astype(jnp.bfloat16)
                for row in range(rows):
                    out_ref[row * heads + pair * 2 + side, part * slots : (part + 1) * slots, :] = (
                        packed[row * slots : (row + 1) * slots]
                    )
        block = pl.ds(part * slots, slots)
        copies.append(
            pltpu.make_async_copy(out_ref.at[:, block], out_hbm.at[:, block], sems.at[part])
        )
        copies[part].start()
    for copy in copies:
        copy.wait()


def packed_part(ref, index):
    chips, third, _ = ref.shape
    slots = third // 3
    return ref[:, index * slots : (index + 1) * slots, :].reshape(chips * slots, PAIR)


def attend(for_own, for_peer, key_own, key_peer, values, out_ref):
    scores = jnp.concatenate([dot_t(for_own, key_own), dot_t(for_peer, key_peer)], axis=1)
    weights = jnp.exp(scores - jnp.max(scores, axis=-1, keepdims=True))
    total = jnp.sum(weights, axis=-1, keepdims=True)
    mixed = dot(weights.astype(jnp.bfloat16), values) / total
    out_ref[...] = mixed.astype(jnp.bfloat16).reshape(out_ref.shape)


def lane_masks(tokens):
    lane = lax.broadcasted_iota(jnp.int32, (tokens, PAIR), 1)
    bf16 = jnp.bfloat16
    return lane < HEAD_DIM, (lane == 0).astype(bf16), (lane == HEAD_DIM).astype(bf16)


def axial_peer_kernel(
    in_ref, bias_own_ref, bias_peer_ref, out_ref, key_own_ref, key_peer_ref, values_ref, rolled_ref
):
    tokens = bias_own_ref.shape[0]
    low, low_one, high_one = lane_masks(tokens)
    query, key, value = (packed_part(in_ref, index) for index in range(3))
    key_own_ref[...] = jnp.where(low, key, bias_own_ref[...])
    key_peer_ref[...] = jnp.where(low, bias_peer_ref[...], key)
    query_rolled, value_rolled = half_roll(query), half_roll(value)
    values_ref[:tokens] = value
    values_ref[tokens:] = value_rolled
    rolled_ref[...] = query_rolled
    attend(
        jnp.where(low, query_rolled, high_one),
        jnp.where(low, low_one, query),
        key_own_ref[...],
        key_peer_ref[...],
        jnp.concatenate([value_rolled, value], axis=0),
        out_ref,
    )


def axial_own_kernel(in_ref, key_own_ref, key_peer_ref, values_ref, rolled_ref, out_ref):
    low, low_one, high_one = lane_masks(rolled_ref.shape[0])
    attend(
        jnp.where(low, packed_part(in_ref, 0), high_one),
        jnp.where(low, low_one, rolled_ref[...]),
        key_own_ref[...],
        key_peer_ref[...],
        values_ref[...],
        out_ref,
    )


def join_kernel(low_ref, high_ref, out_ref):
    items, slots, _ = out_ref.shape
    low = low_half((items * slots, PAIR))
    joined = jnp.where(
        low, low_ref[...].reshape(items * slots, PAIR), high_ref[...].reshape(items * slots, PAIR)
    )
    out_ref[...] = joined.reshape(out_ref.shape)


def band_kernel(
    lat_count, lon_count, points_ref, mask_ref, own_ref, below_ref, above_ref, below2_ref, above2_ref,
    wq_hbm, wk_hbm, wv_hbm, fields_hbm, w_hbm,
    out_ref, axial_w_ref, bias_own_ref, bias_peer_ref,
    weights_ref, fields_ref, w_ref, band_ref, sems,
):
    first = AXIAL_HEADS * HEAD_DIM
    columns = pl.ds(first, weights_ref.shape[2])
    copies = [
        pltpu.make_async_copy(hbm.at[:, columns], weights_ref.at[place], sems.at[place])
        for place, hbm in enumerate((wk_hbm, wv_hbm, wq_hbm))
    ]
    late = [
        pltpu.make_async_copy(w_hbm.at[pl.ds(first, w_ref.shape[0])], w_ref, sems.at[3]),
        pltpu.make_async_copy(fields_hbm, fields_ref, sems.at[4]),
    ]
    lat = lax.axis_index("lat")
    lon = lax.axis_index("lon")
    core = lax.rem(lon, 2)
    heads = AXIAL_HEADS // 2
    for head in range(heads):
        for side in range(2):
            source = (jnp.where(side == 0, core, 1 - core) * heads + head) * HEAD_DIM
            late.append(
                pltpu.make_async_copy(
                    w_hbm.at[pl.ds(pl.multiple_of(source, HEAD_DIM), HEAD_DIM)],
                    axial_w_ref.at[pl.ds(head * PAIR + side * HEAD_DIM, HEAD_DIM)],
                    sems.at[5 + head * 2 + side],
                )
            )
    for copy in copies + late:
        copy.start()
    tokens = own_ref.shape[0]
    slots = 32
    rows = tokens // slots
    bf16 = jnp.bfloat16
    own = own_ref[...]
    everything = jnp.concatenate([own, below_ref[...], above_ref[...], below2_ref[...], above2_ref[...]], axis=0)
    keys = everything.shape[0]
    slot = lax.broadcasted_iota(jnp.int32, (slots, PAIR), 0)
    blocks = []
    for offset in (0,) + OFFSETS:
        source = lat + offset
        held = jnp.clip(source, 0, lat_count - 1)
        if offset == 0:
            allowed = jnp.int32(1)
        else:
            column = offset + REACH if offset < 0 else offset + REACH - 1
            inside = (source >= 0) & (source < lat_count)
            allowed = jnp.where(inside & (mask_ref[column, lat] == 1), 1, 0)
        for row in range(rows):
            count = live_count(points_ref[held * rows + row], lon, lon_count) * allowed
            blocks.append(jnp.where(slot < count, 0.0, DEAD))
    bias = jnp.concatenate(blocks, axis=0)
    lane_k = lax.broadcasted_iota(jnp.int32, (keys, PAIR), 1)
    lane_q = lax.broadcasted_iota(jnp.int32, (tokens, PAIR), 1)
    low_k, low_q = lane_k < HEAD_DIM, lane_q < HEAD_DIM
    bias_high = jnp.where(lane_k == HEAD_DIM, bias, 0.0).astype(bf16)
    bias_low = jnp.where(lane_k == 0, bias, 0.0).astype(bf16)
    one_high = (lane_q == HEAD_DIM).astype(bf16)
    one_low = (lane_q == 0).astype(bf16)
    copies[0].wait()
    key = dot(everything, weights_ref[0]).astype(bf16)
    copies[1].wait()
    value = dot(everything, weights_ref[1]).astype(bf16)
    copies[2].wait()
    query = dot(own, weights_ref[2]).astype(bf16) * bf16(SCALE)
    for pair in range((HEADS - AXIAL_HEADS) // 2):
        span = slice(pair * PAIR, (pair + 1) * PAIR)
        q, k, v = query[:, span], key[:, span], value[:, span]
        scores = jnp.concatenate(
            [
                dot_t(jnp.where(low_q, q, one_high), jnp.where(low_k, k, bias_high)),
                dot_t(jnp.where(low_q, one_low, q), jnp.where(low_k, bias_low, k)),
            ],
            axis=0,
        )
        weights = jnp.exp(scores - jnp.max(scores, axis=-1, keepdims=True))
        total = jnp.sum(weights, axis=-1, keepdims=True)
        mixed = dot(weights.astype(bf16), v) / total
        band_ref[:, span] = jnp.where(low_q, mixed[:tokens], mixed[tokens:]).astype(bf16)
    order = chip_order(lon_count // 2)
    points = points_ref[lat * rows + place_of(lon // 2, len(order)) // heads]
    lane = lax.broadcasted_iota(jnp.int32, (slots, PAIR), 1)
    for place, source in enumerate(order):
        part = pl.ds(place * slots, slots)
        dead_own = slot >= live_count(points, 2 * source + core, lon_count)
        dead_peer = slot >= live_count(points, 2 * source + 1 - core, lon_count)
        bias_own_ref[part, :] = jnp.where(dead_own & (lane == HEAD_DIM), DEAD, 0.0).astype(bf16)
        bias_peer_ref[part, :] = jnp.where(dead_peer & (lane == 0), DEAD, 0.0).astype(bf16)
    for copy in late[:2]:
        copy.wait()
    width = fields_ref.shape[2]
    out_ref[...] = fields_ref[...].reshape(tokens, width) + dot(band_ref[...], w_ref[...])
    for copy in late[2:]:
        copy.wait()


def finish_kernel(lon_count, points_ref, sum_ref, mixed_ref, w_ref, out_hbm, out_ref, sems):
    lon = lax.axis_index("lon")
    lat = lax.axis_index("lat")
    rows, slots, width = out_ref.shape
    heads = AXIAL_HEADS // 2
    mixed = jnp.concatenate(
        [
            jnp.concatenate([mixed_ref[row * heads + head] for head in range(heads)], axis=1)
            for row in range(rows)
        ],
        axis=0,
    )
    step = 256
    slot = lax.broadcasted_iota(jnp.int32, (slots, step), 0)
    counts = [live_count(points_ref[lat * rows + row], lon, lon_count) for row in range(rows)]
    copies = []
    for place in range(width // step):
        span = pl.ds(place * step, step)
        result = sum_ref[:, span] + dot(mixed, w_ref[:, span])
        for row in range(rows):
            out_ref[row, :, span] = jnp.where(
                slot < counts[row], result[row * slots : (row + 1) * slots], 0.0
            )
        copies.append(
            pltpu.make_async_copy(out_ref.at[:, :, span], out_hbm.at[:, :, span], sems.at[place])
        )
        copies[place].start()
    for copy in copies:
        copy.wait()


def call(kernel, shapes, specs, scratch=(), flops=0, out=VMEM):
    return pl.pallas_call(
        kernel,
        out_shape=[jax.ShapeDtypeStruct(shape, dtype) for shape, dtype in shapes],
        in_specs=specs,
        out_specs=[out] * len(shapes),
        scratch_shapes=scratch,
        compiler_params=pltpu.CompilerParams(vmem_limit_bytes=24 * 1024 * 1024),
        cost_estimate=pl.CostEstimate(flops=flops, transcendentals=0, bytes_accessed=0) if flops else None,
    )


def on_device(fields, row_points, band_mask, norm_gain, w_query, w_key, w_value, w_out):
    rows, slots, width = fields.shape
    lat_count = lax.axis_size("lat")
    lon_count = lax.axis_size("lon")
    tokens = rows * slots
    chips = lon_count // 2
    axial_width = AXIAL_HEADS * HEAD_DIM
    band_width = (HEADS - AXIAL_HEADS) * HEAD_DIM
    bf16, f32 = jnp.bfloat16, jnp.float32
    groups = [[2 * chip + core for chip in chip_order(chips)] for core in range(2)]
    swap = [(place, place + 1 - 2 * (place % 2)) for place in range(lon_count)]

    def in_hbm(*arrays):
        return [pltpu.with_memory_space_constraint(array, pltpu.HBM) for array in arrays]

    normed, weights = call(
        norm_kernel,
        [((tokens, width), bf16), ((3, width, axial_width // 2), bf16)],
        [HBM] * 5,
        [
            pltpu.VMEM((rows, slots, width), f32),
            pltpu.VMEM((1, width), f32),
            pltpu.SemaphoreType.DMA((4 + rows,)),
        ],
    )(*in_hbm(fields, norm_gain.reshape(1, width), w_query, w_key, w_value))
    peer = lax.ppermute(normed, "lon", swap)
    near = [
        lax.ppermute(
            normed, "lat", [(place, (place - offset) % lat_count) for place in range(lat_count)]
        )
        for offset in OFFSETS
    ]
    (packed,) = call(
        axial_project_kernel,
        [((chips, 3 * slots, PAIR), bf16)],
        [VMEM] * 3,
        [pltpu.VMEM((chips, 3 * slots, PAIR), bf16), pltpu.SemaphoreType.DMA((3,))],
        out=ANY,
    )(normed, peer, weights)
    row_head = lax.all_to_all(packed, "lon", 0, 0, axis_index_groups=groups, tiled=True)
    wide = ((chips * slots, PAIR), bf16)
    summed, axial_w, bias_own, bias_peer = call(
        functools.partial(band_kernel, lat_count, lon_count),
        [((tokens, width), f32), ((axial_width, width), bf16), wide, wide],
        [SMEM, SMEM] + [VMEM] * 5 + [HBM] * 5,
        [
            pltpu.VMEM((3, width, band_width), bf16),
            pltpu.VMEM((rows, slots, width), f32),
            pltpu.VMEM((band_width, width), bf16),
            pltpu.VMEM((tokens, band_width), bf16),
            pltpu.SemaphoreType.DMA((5 + AXIAL_HEADS,)),
        ],
        BAND_FLOPS,
    )(row_points, band_mask.T, normed, *near, *in_hbm(w_query, w_key, w_value, fields, w_out))
    item = ((chips, slots, PAIR), bf16)
    away, key_own, key_peer, values, rolled = call(
        axial_peer_kernel,
        [item, wide, wide, ((2 * chips * slots, PAIR), bf16), wide],
        [VMEM] * 3,
    )(row_head, bias_own, bias_peer)
    arrived = lax.ppermute(away, "lon", swap)
    (home,) = call(axial_own_kernel, [item], [VMEM] * 5, flops=AXIAL_FLOPS)(
        row_head, key_own, key_peer, values, rolled
    )
    (joined,) = call(join_kernel, [item], [VMEM] * 2)(home, arrived)
    mixed = lax.all_to_all(joined, "lon", 0, 0, axis_index_groups=groups, tiled=True)
    (out,) = call(
        functools.partial(finish_kernel, lon_count),
        [((rows, slots, width), f32)],
        [SMEM] + [VMEM] * 3,
        [pltpu.VMEM((rows, slots, width), f32), pltpu.SemaphoreType.DMA((4,))],
        out=ANY,
    )(row_points, summed, mixed, axial_w)
    return out


def solution(mesh):
    in_specs = (P("lat", "lon", None), P(), P(), P(), P(), P(), P(), P())
    out_specs = P("lat", "lon", None)
    return jax.shard_map(
        on_device, mesh=mesh, in_specs=in_specs, out_specs=out_specs, check_vma=False
    )
```

```python
import functools

import jax
import jax.numpy as jnp
from jax import lax
from jax.experimental import pallas as pl
from jax.experimental.pallas import tpu as pltpu
from jax.sharding import PartitionSpec as P

HEADS = 16
HEAD_DIM = 64
AXIAL_HEADS = 8
REACH = 2
EPS = 1e-05
DEAD = -1e30
PAIR = 2 * HEAD_DIM
SCALE = HEAD_DIM**-0.5
OFFSETS = (-1, -2, 2, 1)
AXIAL_FLOPS = 20_000_000_000
BAND_FLOPS = 20_000_000_000

VMEM = pl.BlockSpec(memory_space=pltpu.VMEM)
SMEM = pl.BlockSpec(memory_space=pltpu.SMEM)
HBM = pl.BlockSpec(memory_space=pltpu.HBM)
ANY = pl.BlockSpec(memory_space=pl.ANY)


def dot(a, b):
    return jnp.dot(a, b, preferred_element_type=jnp.float32)


def dot_t(a, b):
    return lax.dot_general(a, b, (((1,), (1,)), ((), ())), preferred_element_type=jnp.float32)


def half_roll(value):
    return pltpu.roll(value, HEAD_DIM, 1)


def low_half(shape):
    return lax.broadcasted_iota(jnp.int32, shape, 1) < HEAD_DIM


def chip_order(chips):
    half = chips // 2
    return [side * half + (z + half // 2) % half for side in (1, 0) for z in range(half)]


def place_of(chip, chips):
    half = chips // 2
    return (1 - chip // half) * half + lax.rem(lax.rem(chip, half) + half // 2, half)


def live_count(points, tile, tiles):
    return points // tiles + (tile < points % tiles).astype(jnp.int32)


def norm_kernel(
    fields_hbm, gain_hbm, wq_hbm, wk_hbm, wv_hbm, out_ref, weights_ref, fields_ref, gain_ref, sems
):
    core = lax.rem(lax.axis_index("lon"), 2)
    width = weights_ref.shape[2]
    columns = pl.ds(pl.multiple_of(core * width, width), width)
    rows = fields_hbm.shape[0]
    slots = fields_hbm.shape[1]
    gain_copy = pltpu.make_async_copy(gain_hbm, gain_ref, sems.at[0])
    row_copies = [
        pltpu.make_async_copy(fields_hbm.at[row], fields_ref.at[row], sems.at[1 + row])
        for row in range(rows)
    ]
    rest = [
        pltpu.make_async_copy(hbm.at[:, columns], weights_ref.at[place], sems.at[1 + rows + place])
        for place, hbm in enumerate((wq_hbm, wk_hbm, wv_hbm))
    ]
    for copy in [gain_copy] + row_copies + rest:
        copy.start()
    gain_copy.wait()
    for row in range(rows):
        row_copies[row].wait()
        values = fields_ref[row]
        mean = jnp.mean(values, axis=-1, keepdims=True)
        centred = values - mean
        var = jnp.mean(centred * centred, axis=-1, keepdims=True)
        out_ref[row * slots : (row + 1) * slots, :] = (
            centred * lax.rsqrt(var + EPS) * gain_ref[...]
        ).astype(jnp.bfloat16)
    for copy in rest:
        copy.wait()


def axial_project_kernel(own_ref, peer_ref, weights_ref, out_hbm, out_ref, sems):
    tokens = own_ref.shape[0]
    items, third, _ = out_ref.shape
    slots = third // 3
    rows = tokens // slots
    heads = AXIAL_HEADS // 2
    both = jnp.concatenate([own_ref[...], peer_ref[...]], axis=0)
    low = low_half((tokens, PAIR))
    copies = []
    for part in range(3):
        result = dot(both, weights_ref[part])
        if part == 0:
            result = result.astype(jnp.bfloat16).astype(jnp.float32) * SCALE
        for pair in range(heads // 2):
            span = slice(pair * PAIR, (pair + 1) * PAIR)
            own, peer = result[:tokens, span], result[tokens:, span]
            sides = (
                jnp.where(low, own, half_roll(peer)),
                jnp.where(low, half_roll(own), peer),
            )
            for side in range(2):
                packed = sides[side].astype(jnp.bfloat16)
                for row in range(rows):
                    out_ref[row * heads + pair * 2 + side, part * slots : (part + 1) * slots, :] = (
                        packed[row * slots : (row + 1) * slots]
                    )
        block = pl.ds(part * slots, slots)
        copies.append(
            pltpu.make_async_copy(out_ref.at[:, block], out_hbm.at[:, block], sems.at[part])
        )
        copies[part].start()
    for copy in copies:
        copy.wait()


def packed_part(ref, index):
    chips, third, _ = ref.shape
    slots = third // 3
    return ref[:, index * slots : (index + 1) * slots, :].reshape(chips * slots, PAIR)


def attend(for_own, for_peer, key_own, key_peer, values, out_ref):
    scores = jnp.concatenate([dot_t(for_own, key_own), dot_t(for_peer, key_peer)], axis=1)
    weights = jnp.exp(scores - jnp.max(scores, axis=-1, keepdims=True))
    total = jnp.sum(weights, axis=-1, keepdims=True)
    mixed = dot(weights.astype(jnp.bfloat16), values) / total
    out_ref[...] = mixed.astype(jnp.bfloat16).reshape(out_ref.shape)


def lane_masks(tokens):
    lane = lax.broadcasted_iota(jnp.int32, (tokens, PAIR), 1)
    bf16 = jnp.bfloat16
    return lane < HEAD_DIM, (lane == 0).astype(bf16), (lane == HEAD_DIM).astype(bf16)


def axial_peer_kernel(
    in_ref, bias_own_ref, bias_peer_ref, out_ref, key_own_ref, key_peer_ref, values_ref, rolled_ref
):
    tokens = bias_own_ref.shape[0]
    low, low_one, high_one = lane_masks(tokens)
    query, key, value = (packed_part(in_ref, index) for index in range(3))
    key_own_ref[...] = jnp.where(low, key, bias_own_ref[...])
    key_peer_ref[...] = jnp.where(low, bias_peer_ref[...], key)
    query_rolled, value_rolled = half_roll(query), half_roll(value)
    values_ref[:tokens] = value
    values_ref[tokens:] = value_rolled
    rolled_ref[...] = query_rolled
    attend(
        jnp.where(low, query_rolled, high_one),
        jnp.where(low, low_one, query),
        key_own_ref[...],
        key_peer_ref[...],
        jnp.concatenate([value_rolled, value], axis=0),
        out_ref,
    )


def axial_own_kernel(in_ref, key_own_ref, key_peer_ref, values_ref, rolled_ref, out_ref):
    low, low_one, high_one = lane_masks(rolled_ref.shape[0])
    attend(
        jnp.where(low, packed_part(in_ref, 0), high_one),
        jnp.where(low, low_one, rolled_ref[...]),
        key_own_ref[...],
        key_peer_ref[...],
        values_ref[...],
        out_ref,
    )


def join_kernel(low_ref, high_ref, out_ref):
    items, slots, _ = out_ref.shape
    low = low_half((items * slots, PAIR))
    joined = jnp.where(
        low, low_ref[...].reshape(items * slots, PAIR), high_ref[...].reshape(items * slots, PAIR)
    )
    out_ref[...] = joined.reshape(out_ref.shape)


def band_kernel(
    lat_count, lon_count, points_ref, mask_ref, own_ref, below_ref, below2_ref, above2_ref, above_ref,
    wq_hbm, wk_hbm, wv_hbm, fields_hbm, w_hbm,
    out_ref, axial_w_ref, bias_own_ref, bias_peer_ref,
    weights_ref, fields_ref, w_ref, band_ref, sems,
):
    first = AXIAL_HEADS * HEAD_DIM
    columns = pl.ds(first, weights_ref.shape[2])
    copies = [
        pltpu.make_async_copy(hbm.at[:, columns], weights_ref.at[place], sems.at[place])
        for place, hbm in enumerate((wk_hbm, wv_hbm, wq_hbm))
    ]
    late = [
        pltpu.make_async_copy(w_hbm.at[pl.ds(first, w_ref.shape[0])], w_ref, sems.at[3]),
        pltpu.make_async_copy(fields_hbm, fields_ref, sems.at[4]),
    ]
    lat = lax.axis_index("lat")
    lon = lax.axis_index("lon")
    core = lax.rem(lon, 2)
    heads = AXIAL_HEADS // 2
    for head in range(heads):
        for side in range(2):
            source = (jnp.where(side == 0, core, 1 - core) * heads + head) * HEAD_DIM
            late.append(
                pltpu.make_async_copy(
                    w_hbm.at[pl.ds(pl.multiple_of(source, HEAD_DIM), HEAD_DIM)],
                    axial_w_ref.at[pl.ds(head * PAIR + side * HEAD_DIM, HEAD_DIM)],
                    sems.at[5 + head * 2 + side],
                )
            )
    for copy in copies + late:
        copy.start()
    tokens = own_ref.shape[0]
    slots = 32
    rows = tokens // slots
    bf16 = jnp.bfloat16
    own = own_ref[...]
    everything = jnp.concatenate([own, below_ref[...], below2_ref[...], above2_ref[...], above_ref[...]], axis=0)
    keys = everything.shape[0]
    slot = lax.broadcasted_iota(jnp.int32, (slots, PAIR), 0)
    blocks = []
    for offset in (0,) + OFFSETS:
        source = lat + offset
        held = jnp.clip(source, 0, lat_count - 1)
        if offset == 0:
            allowed = jnp.int32(1)
        else:
            column = offset + REACH if offset < 0 else offset + REACH - 1
            inside = (source >= 0) & (source < lat_count)
            allowed = jnp.where(inside & (mask_ref[column, lat] == 1), 1, 0)
        for row in range(rows):
            count = live_count(points_ref[held * rows + row], lon, lon_count) * allowed
            blocks.append(jnp.where(slot < count, 0.0, DEAD))
    bias = jnp.concatenate(blocks, axis=0)
    lane_k = lax.broadcasted_iota(jnp.int32, (keys, PAIR), 1)
    lane_q = lax.broadcasted_iota(jnp.int32, (tokens, PAIR), 1)
    low_k, low_q = lane_k < HEAD_DIM, lane_q < HEAD_DIM
    bias_high = jnp.where(lane_k == HEAD_DIM, bias, 0.0).astype(bf16)
    bias_low = jnp.where(lane_k == 0, bias, 0.0).astype(bf16)
    one_high = (lane_q == HEAD_DIM).astype(bf16)
    one_low = (lane_q == 0).astype(bf16)
    copies[0].wait()
    key = dot(everything, weights_ref[0]).astype(bf16)
    copies[1].wait()
    value = dot(everything, weights_ref[1]).astype(bf16)
    copies[2].wait()
    query = dot(own, weights_ref[2]).astype(bf16) * bf16(SCALE)
    for pair in range((HEADS - AXIAL_HEADS) // 2):
        span = slice(pair * PAIR, (pair + 1) * PAIR)
        q, k, v = query[:, span], key[:, span], value[:, span]
        scores = jnp.concatenate(
            [
                dot_t(jnp.where(low_q, q, one_high), jnp.where(low_k, k, bias_high)),
                dot_t(jnp.where(low_q, one_low, q), jnp.where(low_k, bias_low, k)),
            ],
            axis=0,
        )
        weights = jnp.exp(scores - jnp.max(scores, axis=-1, keepdims=True))
        total = jnp.sum(weights, axis=-1, keepdims=True)
        mixed = dot(weights.astype(bf16), v) / total
        band_ref[:, span] = jnp.where(low_q, mixed[:tokens], mixed[tokens:]).astype(bf16)
    order = chip_order(lon_count // 2)
    points = points_ref[lat * rows + place_of(lon // 2, len(order)) // heads]
    lane = lax.broadcasted_iota(jnp.int32, (slots, PAIR), 1)
    for place, source in enumerate(order):
        part = pl.ds(place * slots, slots)
        dead_own = slot >= live_count(points, 2 * source + core, lon_count)
        dead_peer = slot >= live_count(points, 2 * source + 1 - core, lon_count)
        bias_own_ref[part, :] = jnp.where(dead_own & (lane == HEAD_DIM), DEAD, 0.0).astype(bf16)
        bias_peer_ref[part, :] = jnp.where(dead_peer & (lane == 0), DEAD, 0.0).astype(bf16)
    for copy in late[:2]:
        copy.wait()
    width = fields_ref.shape[2]
    out_ref[...] = fields_ref[...].reshape(tokens, width) + dot(band_ref[...], w_ref[...])
    for copy in late[2:]:
        copy.wait()


def finish_kernel(lon_count, points_ref, sum_ref, mixed_ref, w_ref, out_hbm, out_ref, sems):
    lon = lax.axis_index("lon")
    lat = lax.axis_index("lat")
    rows, slots, width = out_ref.shape
    heads = AXIAL_HEADS // 2
    mixed = jnp.concatenate(
        [
            jnp.concatenate([mixed_ref[row * heads + head] for head in range(heads)], axis=1)
            for row in range(rows)
        ],
        axis=0,
    )
    step = 256
    slot = lax.broadcasted_iota(jnp.int32, (slots, step), 0)
    counts = [live_count(points_ref[lat * rows + row], lon, lon_count) for row in range(rows)]
    copies = []
    for place in range(width // step):
        span = pl.ds(place * step, step)
        result = sum_ref[:, span] + dot(mixed, w_ref[:, span])
        for row in range(rows):
            out_ref[row, :, span] = jnp.where(
                slot < counts[row], result[row * slots : (row + 1) * slots], 0.0
            )
        copies.append(
            pltpu.make_async_copy(out_ref.at[:, :, span], out_hbm.at[:, :, span], sems.at[place])
        )
        copies[place].start()
    for copy in copies:
        copy.wait()


def call(kernel, shapes, specs, scratch=(), flops=0, out=VMEM):
    return pl.pallas_call(
        kernel,
        out_shape=[jax.ShapeDtypeStruct(shape, dtype) for shape, dtype in shapes],
        in_specs=specs,
        out_specs=[out] * len(shapes),
        scratch_shapes=scratch,
        compiler_params=pltpu.CompilerParams(vmem_limit_bytes=24 * 1024 * 1024),
        cost_estimate=pl.CostEstimate(flops=flops, transcendentals=0, bytes_accessed=0) if flops else None,
    )


def on_device(fields, row_points, band_mask, norm_gain, w_query, w_key, w_value, w_out):
    rows, slots, width = fields.shape
    lat_count = lax.axis_size("lat")
    lon_count = lax.axis_size("lon")
    tokens = rows * slots
    chips = lon_count // 2
    axial_width = AXIAL_HEADS * HEAD_DIM
    band_width = (HEADS - AXIAL_HEADS) * HEAD_DIM
    bf16, f32 = jnp.bfloat16, jnp.float32
    groups = [[2 * chip + core for chip in chip_order(chips)] for core in range(2)]
    swap = [(place, place + 1 - 2 * (place % 2)) for place in range(lon_count)]

    def in_hbm(*arrays):
        return [pltpu.with_memory_space_constraint(array, pltpu.HBM) for array in arrays]

    normed, weights = call(
        norm_kernel,
        [((tokens, width), bf16), ((3, width, axial_width // 2), bf16)],
        [HBM] * 5,
        [
            pltpu.VMEM((rows, slots, width), f32),
            pltpu.VMEM((1, width), f32),
            pltpu.SemaphoreType.DMA((4 + rows,)),
        ],
    )(*in_hbm(fields, norm_gain.reshape(1, width), w_query, w_key, w_value))
    peer = lax.ppermute(normed, "lon", swap)
    near = [
        lax.ppermute(
            normed, "lat", [(place, (place - offset) % lat_count) for place in range(lat_count)]
        )
        for offset in OFFSETS
    ]
    (packed,) = call(
        axial_project_kernel,
        [((chips, 3 * slots, PAIR), bf16)],
        [VMEM] * 3,
        [pltpu.VMEM((chips, 3 * slots, PAIR), bf16), pltpu.SemaphoreType.DMA((3,))],
        out=ANY,
    )(normed, peer, weights)
    row_head = lax.all_to_all(packed, "lon", 0, 0, axis_index_groups=groups, tiled=True)
    wide = ((chips * slots, PAIR), bf16)
    summed, axial_w, bias_own, bias_peer = call(
        functools.partial(band_kernel, lat_count, lon_count),
        [((tokens, width), f32), ((axial_width, width), bf16), wide, wide],
        [SMEM, SMEM] + [VMEM] * 5 + [HBM] * 5,
        [
            pltpu.VMEM((3, width, band_width), bf16),
            pltpu.VMEM((rows, slots, width), f32),
            pltpu.VMEM((band_width, width), bf16),
            pltpu.VMEM((tokens, band_width), bf16),
            pltpu.SemaphoreType.DMA((5 + AXIAL_HEADS,)),
        ],
        BAND_FLOPS,
    )(row_points, band_mask.T, normed, *near, *in_hbm(w_query, w_key, w_value, fields, w_out))
    item = ((chips, slots, PAIR), bf16)
    away, key_own, key_peer, values, rolled = call(
        axial_peer_kernel,
        [item, wide, wide, ((2 * chips * slots, PAIR), bf16), wide],
        [VMEM] * 3,
    )(row_head, bias_own, bias_peer)
    arrived = lax.ppermute(away, "lon", swap)
    (home,) = call(axial_own_kernel, [item], [VMEM] * 5, flops=AXIAL_FLOPS)(
        row_head, key_own, key_peer, values, rolled
    )
    (joined,) = call(join_kernel, [item], [VMEM] * 2)(home, arrived)
    mixed = lax.all_to_all(joined, "lon", 0, 0, axis_index_groups=groups, tiled=True)
    (out,) = call(
        functools.partial(finish_kernel, lon_count),
        [((rows, slots, width), f32)],
        [SMEM] + [VMEM] * 3,
        [pltpu.VMEM((rows, slots, width), f32), pltpu.SemaphoreType.DMA((4,))],
        out=ANY,
    )(row_points, summed, mixed, axial_w)
    return out


def solution(mesh):
    in_specs = (P("lat", "lon", None), P(), P(), P(), P(), P(), P(), P())
    out_specs = P("lat", "lon", None)
    return jax.shard_map(
        on_device, mesh=mesh, in_specs=in_specs, out_specs=out_specs, check_vma=False
    )
```
